32 devices in a mesh: section: 2 (over core), shard: 16 (over z, y, x).
Axes of the slice: x: 2, y: 2, z: 4, core: 2. Of those that a mesh axis runs over, the one named last changes fastest.
Arguments:
- tokens: bfloat16 [2, 1024, 2048], P(None, 'shard'), may hold values from -6 to 6
- cotangent: bfloat16 [2, 1024, 2048], P(None, 'shard'), may hold values from -6 to 6
- block_ids: int32 [2, 1024], replicated, may hold values from 0 to 7, never falling along the last dimension, each value on 1 to 256 neighbouring positions
- token_ids: int32 [2, 1024], P(None, 'shard'), may hold values from 0 to 65535
- attn_weight: bfloat16 [2, 5760, 2048], P('section', 'shard'), may hold values from -0.125 to 0.125
- ff_weight: bfloat16 [2, 3, 8192, 2048], P('section', None, 'shard'), may hold values from -0.125 to 0.125
- gains: bfloat16 [2, 12800], P('section', 'shard'), may hold values from 0.5 to 1.5
- table: bfloat16 [2, 65536, 256], P('section', 'shard'), may hold values from -6 to 6
Outputs:
- layer_outputs: bfloat16 [2, 2, 1024, 2048], P('section', None, 'shard')
- input_grads: bfloat16 [2, 2, 1024, 2048], P('section', None, 'shard')
- attn_grad: float32 [2, 5760, 2048], P('section', 'shard')
- ff_grad: float32 [2, 3, 8192, 2048], P('section', None, 'shard')
- gain_grad: float32 [2, 12800], P('section', 'shard')
- table_grad: float32 [2, 65536, 256], P('section', 'shard')
The draws below stay inside these ranges and needn't reach their ends.
Inputs may be any that keep to these rules, and one draw needn't show every extreme that they name: `block_ids`: along each sequence the block numbers never fall; every block holds 1 to 256 positions and some block exactly 256.
All inputs are finite; a program needn't handle non-finite values.
Results may differ from the reference program's by a relative error of at most 0.022.
Values may be sent and summed in bfloat16 or wider, within the bound.
No kernel may reach another device: no remote copies, remote signals or barrier semaphores. Data moves between devices by JAX's collectives and lax.ppermute only.
A program may use at most 512 MiB of HBM per device.

```python
import math
from functools import partial
import jax
import jax.numpy as jnp
import numpy as np
from jax import lax

D = 2048
FF = 8192
HEADS = 8
KV_HEADS = 2
HEAD_DIM = 256
RANK = 64
PLD = 256
MICRO = 2
BLOCK = 256
LAYERS = 2
SEQ = 1024
VOCAB = 65536
AROWS = 5760
GAINS = 12800


def place_ends(array, key, smallest, high):
    longest = array.shape.index(max(array.shape))
    spots = []
    for shift in (0, 1):
        where = [jax.random.randint(jax.random.fold_in(key, axis), (), 0, length) for axis, length in enumerate(array.shape)]
        where[longest] = (where[longest] + shift) % array.shape[longest]
        spots.append(tuple(where))
    return array.at[spots[0]].set(smallest).at[spots[1]].set(high)


def shard_levels(key, shape, pieces, low, largest):
    level = 1.0
    for position, parts in pieces:
        steps = jax.random.uniform(jax.random.fold_in(jax.random.fold_in(key, 6), position), (parts,), jnp.float32, low / len(pieces), largest / len(pieces))
        level = level * jnp.repeat(jnp.exp(steps), shape[position] // parts).reshape((-1,) + (1,) * (len(shape) - 1 - position))
    return level


def rank_table(count, lean):
    portions = [(1 << 20) // math.isqrt(grade ** lean) + 1 for grade in range(1, count + 1)]
    spread = 1 + sum(portions) // (1 << 30)
    return np.cumsum(np.array([max(1, weight // spread) for weight in portions]))


def ranked_ids(own_key, shape, amount, lean):
    listing = rank_table(amount, lean)
    lot = jax.random.randint(jax.random.fold_in(own_key, 1), shape, 0, int(listing[amount - 1]))
    rank = jnp.searchsorted(jnp.asarray(listing, jnp.int32), lot, side="right")
    return jax.random.permutation(jax.random.fold_in(own_key, 2), amount)[rank].astype(jnp.int32)


def profile(amount, total, bound, slope):
    loads = [(1 << 20) // math.isqrt(grade ** slope) + 1 for grade in range(2, amount + 1)]
    rest, counts = total - bound - (amount - 1), [1] * (amount - 1)
    while rest > 0:
        movable = [i for i in range(amount - 1) if counts[i] < bound]
        mass, remaining = sum([loads[i] for i in movable]), rest
        for i in movable:
            addition = min(bound - counts[i], max(1, remaining * loads[i] // mass), rest)
            counts[i] = counts[i] + addition
            rest = rest - addition
    return np.array([bound] + counts)


def ragged_sizes(stream_key, number_of, total, reach, slope):
    if number_of == 2:
        one = jax.random.randint(stream_key, (), max(1, total - reach), min(reach, total - 1) + 1)
        return jnp.stack([one, total - one])
    lengths = jnp.asarray(profile(number_of, total, reach, slope), jnp.int32)
    twos = (number_of - 1) // 2
    source_of, taker = lengths[1:1 + 2 * twos:2], lengths[2:2 + 2 * twos:2]
    room = jnp.minimum(source_of - 1, reach - taker)
    shifted = jax.random.randint(jax.random.fold_in(stream_key, 1), (twos,), 0, 1 << 20) % (room + 1)
    lengths = lengths.at[1:1 + 2 * twos:2].set(source_of - shifted).at[2:2 + 2 * twos:2].set(taker + shifted)
    return lengths[jax.random.permutation(jax.random.fold_in(stream_key, 2), number_of)]


def bell_draw(stream_key, shape, spread, most, split=(), kind=jnp.bfloat16):
    array = jax.random.normal(stream_key, shape, jnp.float32) * spread
    if len(split) > 0:
        array = shard_levels(stream_key, shape, split, -0.22, 0.18) * array
    return jnp.clip(array, min=-most, max=most).astype(kind)


def setup_inputs(seed: int = 0) -> dict:
    seeds = jax.random.split(jax.random.key(seed), 9)
    return {
        "tokens": bell_draw(seeds[0], (MICRO, SEQ, D), 1.0, 6.0, ((1, 16),)),
        "cotangent": bell_draw(seeds[1], (MICRO, SEQ, D), 1.0, 6.0, ((1, 16),)),
        "block_ids": jax.vmap(lambda own: jnp.searchsorted(jnp.cumsum(ragged_sizes(own, 2 * SEQ // BLOCK, SEQ, BLOCK, 0)), jnp.arange(SEQ), side="right"))(jax.random.split(seeds[2], MICRO)).reshape((MICRO, SEQ)).astype(jnp.int32),
        "token_ids": place_ends(ranked_ids(seeds[3], (MICRO, SEQ), VOCAB, 2), jax.random.fold_in(seeds[3], 3), 0, VOCAB - 1).astype(jnp.int32),
        "attn_weight": bell_draw(seeds[4], (LAYERS, AROWS, D), D ** -0.5, 0.125, ((0, 2), (1, 16))),
        "ff_weight": bell_draw(seeds[5], (LAYERS, 3, FF, D), D ** -0.5, 0.125, ((0, 2), (2, 16))),
        "gains": jnp.clip(1.0 + 0.1 * jax.random.normal(seeds[6], (LAYERS, GAINS), jnp.float32), 0.5, 1.5).astype(jnp.bfloat16),
        "table": bell_draw(seeds[7], (LAYERS, VOCAB, PLD), 1.0, 6.0, ((0, 2), (1, 16))),
    }


EPS = 1e-06
ROPE_BASE = 10000.0
INV_ROOT2 = 0.7071067811865476
MASKED = -1e+30
HIGHEST = lax.Precision.HIGHEST

@jax.custom_vjp
def low(v):
    return lax.optimization_barrier(v.astype(jnp.bfloat16)).astype(jnp.float32)

@jax.custom_vjp
def low_back(v):
    return v

def low_keep(v):
    return (low(v), None)

def low_pass(kept, grad):
    return (grad,)

def back_keep(v):
    return (v, None)

def back_low(kept, grad):
    return (low(grad),)
low.defvjp(low_keep, low_pass)
low_back.defvjp(back_keep, back_low)

def rms_norm(values):
    return values * lax.rsqrt(lax.optimization_barrier(jnp.mean(values * values, axis=-1, keepdims=True)) + EPS)

def scaled_norm(values, gain_vec):
    return rms_norm(values) * gain_vec

def rope_tables(positions):
    half_width = HEAD_DIM // 2
    frequency = ROPE_BASE ** (-jnp.arange(half_width, dtype=jnp.float32) * (2.0 / HEAD_DIM))
    angles = positions.astype(jnp.float32)[:, None] * frequency[None, :]
    return (jnp.cos(angles), jnp.sin(angles))

def rotate(vectors, cosine_part, sine_part):
    half_width = vectors.shape[-1] // 2
    first_half = vectors[..., :half_width]
    second_half = vectors[..., half_width:]
    cosine_rows = cosine_part[:, None, :]
    sine_rows = sine_part[:, None, :]
    return jnp.concatenate([first_half * cosine_rows - second_half * sine_rows, second_half * cosine_rows + first_half * sine_rows], axis=-1)

def split_heads(projected_in, query_gain, key_gain, cosine_part, sine_part):
    row_count = projected_in.shape[0]
    query_width = HEADS * HEAD_DIM
    key_width = KV_HEADS * HEAD_DIM
    queries = projected_in[:, :query_width].reshape(row_count, HEADS, HEAD_DIM)
    key_heads = projected_in[:, query_width:query_width + key_width].reshape(row_count, KV_HEADS, HEAD_DIM)
    value_heads = projected_in[:, query_width + key_width:query_width + 2 * key_width].reshape(row_count, KV_HEADS, HEAD_DIM)
    latent = projected_in[:, query_width + 2 * key_width:]
    queries = rotate(rms_norm(queries) * query_gain, cosine_part, sine_part)
    key_heads = rotate(rms_norm(key_heads) * key_gain, cosine_part, sine_part)
    value_heads = rms_norm(value_heads)
    return (queries, key_heads, value_heads, latent)

def join_piece(hidden_in, normed, attended, laurel_raw, gain_laurel, gain_attn, gain_ffin):
    joined = (hidden_in + rms_norm(attended) * gain_attn + normed + rms_norm(laurel_raw) * gain_laurel) * INV_ROOT2
    return (joined, rms_norm(joined) * gain_ffin)

def gated_gelu(gate_pre, up_pre):
    return jax.nn.gelu(gate_pre, approximate=True) * up_pre

def add_branch(residual, branch, gain_out):
    return residual + rms_norm(branch) * gain_out

def product(left_side, right_side):
    return jnp.dot(left_side, right_side, precision=HIGHEST, preferred_element_type=jnp.float32)

def product_rows(left_side, right_side):
    return lax.dot_general(left_side, right_side, (((1,), (1,)), ((), ())), precision=HIGHEST, preferred_element_type=jnp.float32)

def attend_block(queries, key_heads, value_heads, query_blocks, key_blocks):
    row_count = queries.shape[0]
    grouped = queries.reshape(row_count, KV_HEADS, HEADS // KV_HEADS, HEAD_DIM)
    scores = jnp.einsum('qkgd,jkd->kgqj', grouped, key_heads, precision=HIGHEST, preferred_element_type=jnp.float32) * HEAD_DIM ** (-0.5)
    scores = low_back(scores)
    allowed = key_blocks[None, :] <= query_blocks[:, None]
    scores = jnp.where(allowed, scores, MASKED)
    row_max = lax.optimization_barrier(jnp.max(scores, axis=-1, keepdims=True))
    exponentials = jnp.exp(scores - row_max)
    probabilities = low(exponentials / lax.optimization_barrier(jnp.sum(exponentials, axis=-1, keepdims=True)))
    mixed_heads = jnp.einsum('kgqj,jkd->qkgd', probabilities, value_heads, precision=HIGHEST, preferred_element_type=jnp.float32)
    return mixed_heads.reshape(row_count, HEADS * HEAD_DIM)

def layer_step(hidden_in, per_layer, blocks, attn_w, ff_w, gain_w, cosine_part, sine_part):
    query_width = HEADS * HEAD_DIM
    input_rows = query_width + 2 * KV_HEADS * HEAD_DIM + RANK
    output_start = input_rows + PLD
    laurel_start = output_start + query_width
    side_start = laurel_start + RANK
    gain_rows = gain_w[:6 * D].reshape(6, D)
    query_gain = gain_w[6 * D:6 * D + HEAD_DIM]
    key_gain = gain_w[6 * D + HEAD_DIM:]
    normed = scaled_norm(hidden_in, gain_rows[0])
    projected_in = low_back(product_rows(low(normed), attn_w[:input_rows]))
    queries, key_heads, value_heads, latent = split_heads(projected_in, query_gain, key_gain, cosine_part, sine_part)
    queries = low(queries)
    key_heads = low(key_heads)
    value_heads = low(value_heads)
    block_rows = min(512, SEQ)
    block_count = SEQ // block_rows

    def one_block(block_items):
        return attend_block(block_items[0], key_heads, value_heads, block_items[1], blocks)
    mixed_heads = lax.map(jax.checkpoint(one_block), (queries.reshape(block_count, block_rows, HEADS, HEAD_DIM), blocks.reshape(block_count, block_rows)))
    mixed_heads = low_back(low(mixed_heads.reshape(SEQ, query_width)))
    attended = low_back(product(mixed_heads, attn_w[output_start:laurel_start]))
    laurel_raw = low_back(product(low(latent), attn_w[laurel_start:side_start]))
    joined, prenorm = join_piece(hidden_in, normed, attended, laurel_raw, gain_rows[1], gain_rows[2], gain_rows[3])
    gate_up = low_back(jnp.einsum('rd,cfd->crf', low(prenorm), ff_w[:2], precision=HIGHEST, preferred_element_type=jnp.float32))
    hidden_ff = low(gated_gelu(gate_up[0], gate_up[1]))
    down_out = low_back(product(hidden_ff, ff_w[2]))
    settled = add_branch(joined, down_out, gain_rows[4])
    side_gate = low_back(product_rows(low(settled), attn_w[input_rows:output_start]))
    gated_side = low(gated_gelu(side_gate, per_layer))
    projected = low_back(product(gated_side, attn_w[side_start:]))
    return add_branch(settled, projected, gain_rows[5])

def reference(tokens, cotangent, block_ids, token_ids, attn_weight, ff_weight, gains, table):
    cosine_part, sine_part = rope_tables(jnp.arange(SEQ, dtype=jnp.int32))
    token_values = tokens.astype(jnp.float32)

    def forward(attn_all, ff_all, gain_all, table_all, probe_all):
        rounded_outs = []
        carried = token_values + probe_all[0]
        for layer_index in range(LAYERS):
            if layer_index > 0:
                carried = low_back(rounded_outs[-1] + probe_all[layer_index])
            per_layer = low_back(table_all[layer_index][token_ids])
            layer_call = jax.checkpoint(partial(layer_step, attn_w=attn_all[layer_index], ff_w=ff_all[layer_index], gain_w=gain_all[layer_index], cosine_part=cosine_part, sine_part=sine_part))

            def scan_body(carry_state, scan_items, layer_call=layer_call):
                return (carry_state, layer_call(scan_items[0], scan_items[1], scan_items[2]))
            final_state, layer_out = lax.scan(scan_body, jnp.zeros((), jnp.float32), (carried, per_layer, block_ids))
            rounded_outs.append(low(layer_out))
        return jnp.stack(rounded_outs)
    outputs, pullback = jax.vjp(forward, attn_weight.astype(jnp.float32), ff_weight.astype(jnp.float32), gains.astype(jnp.float32), table.astype(jnp.float32), jnp.zeros((LAYERS, MICRO, SEQ, D), jnp.float32))
    seed_grad = jnp.zeros_like(outputs).at[LAYERS - 1].set(cotangent.astype(jnp.float32))
    grad_attn, grad_ff, grad_gain, grad_table, grad_probe = pullback(seed_grad)
    return (outputs.astype(jnp.bfloat16), grad_probe.astype(jnp.bfloat16), grad_attn, grad_ff, grad_gain, grad_table)
```

```python
import itertools
import math
from functools import partial

import jax
import jax.numpy as jnp
from jax import lax
from jax.sharding import PartitionSpec as P

D = 2048
HEADS = 8
KV_HEADS = 2
HEAD_DIM = 256
RANK = 64
PLD = 256
HALF = D // 2
QW = HEADS * HEAD_DIM
KW = KV_HEADS * HEAD_DIM
IN_ROWS = QW + 2 * KW + RANK
OUT_START = IN_ROWS + PLD
LAUREL_START = OUT_START + QW
SIDE_START = LAUREL_START + RANK

EPS = 1e-06
ROPE_BASE = 10000.0
INV_ROOT2 = 0.7071067811865476
MASKED = -1e30
SCALE = HEAD_DIM ** (-0.5)
BF = jnp.bfloat16
F32 = jnp.float32

ZXY = (0, 2, 1)
ZYX = (0, 1, 2)
ZY = (0, 1)
X_ONLY = (2,)


def chip_dims(n):
    side = math.isqrt(n // 4)
    return (4, side, side)


def ring_pairs(n, dim, step):
    sizes = chip_dims(n)
    stride = (sizes[1] * sizes[2], sizes[2], 1)[dim]
    pairs = []
    for i in range(n):
        place = (i // stride) % sizes[dim]
        pairs.append((i, i + ((place + step) % sizes[dim] - place) * stride))
    return pairs


def hop(value, n, dim, step):
    return lax.ppermute(value, "shard", ring_pairs(n, dim, step))


def swap_cores(value):
    return lax.ppermute(value, "section", [(0, 1), (1, 0)])


def offsets_of(n, order):
    sizes = chip_dims(n)
    return list(itertools.product(*[range(sizes[d]) for d in order]))


def tree(n, order):
    edges = []
    for offset in offsets_of(n, order):
        if sum(offset) == 0:
            continue
        last = max(i for i, steps in enumerate(offset) if steps > 0)
        parent = tuple(steps - (i == last) for i, steps in enumerate(offset))
        edges.append((sum(offset), offset, parent, order[last]))
    return edges


def source_index(me, n, order, offset):
    sizes = chip_dims(n)
    strides = (sizes[1] * sizes[2], sizes[2], 1)
    index = me
    for dim, steps in zip(order, offset):
        place = (me // strides[dim]) % sizes[dim]
        index = index + ((place - steps) % sizes[dim] - place) * strides[dim]
    return index


def gather_tree(pieces, n, fence=True):
    trees = [tree(n, order) for _, order in pieces]
    found = [{(0,) * len(order): block} for block, order in pieces]
    held = [dict(blocks) for blocks in found]
    rounds = max(edge[0] for edges in trees for edge in edges)
    for number in range(1, rounds + 1):
        if fence and number > 1:
            keys = [(p, offset) for p in range(len(pieces)) for offset in held[p]]
            values = lax.optimization_barrier([held[p][offset] for p, offset in keys])
            for (p, offset), value in zip(keys, values):
                held[p][offset] = value
        for p, edges in enumerate(trees):
            for edge_round, offset, parent, dim in edges:
                if edge_round == number:
                    value = hop(held[p][parent], n, dim, 1)
                    found[p][offset] = value
                    held[p][offset] = value
    return found


def scatter_tree(pieces, n, fence=False):
    trees = [tree(n, order) for _, order in pieces]
    sums = [dict(terms) for terms, _ in pieces]
    rounds = max(edge[0] for edges in trees for edge in edges)
    for number in range(rounds, 0, -1):
        todo = [
            (p, offset, parent, dim)
            for p, edges in enumerate(trees)
            for edge_round, offset, parent, dim in edges
            if edge_round == number
        ]
        sends = [sums[p][offset].astype(BF) for p, offset, _, _ in todo]
        if fence:
            sends = lax.optimization_barrier(sends)
        for (p, offset, parent, dim), send in zip(todo, sends):
            sums[p][parent] = sums[p][parent].astype(F32) + hop(send, n, dim, -1).astype(F32)
    return [total[(0,) * len(order)] for total, (_, order) in zip(sums, pieces)]


def rms_norm(values):
    return values * lax.rsqrt(jnp.mean(values * values, axis=-1, keepdims=True) + EPS)


def scaled_norm(values, gain_vec):
    return rms_norm(values) * gain_vec


def rope_tables(positions):
    half_width = HEAD_DIM // 2
    frequency = ROPE_BASE ** (-jnp.arange(half_width, dtype=F32) * (2.0 / HEAD_DIM))
    angles = positions.astype(F32)[:, None] * frequency[None, :]
    return (jnp.cos(angles), jnp.sin(angles))


def rotate(vectors, cosine_part, sine_part):
    half_width = vectors.shape[-1] // 2
    first_half = vectors[..., :half_width]
    second_half = vectors[..., half_width:]
    cosine_rows = cosine_part[:, None, :]
    sine_rows = sine_part[:, None, :]
    return jnp.concatenate(
        [
            first_half * cosine_rows - second_half * sine_rows,
            second_half * cosine_rows + first_half * sine_rows,
        ],
        axis=-1,
    )


def split_heads(projected_in, query_gain, key_gain, cosine_part, sine_part):
    row_count = projected_in.shape[0]
    queries = projected_in[:, :QW].reshape(row_count, HEADS, HEAD_DIM)
    key_heads = projected_in[:, QW : QW + KW].reshape(row_count, KV_HEADS, HEAD_DIM)
    value_heads = projected_in[:, QW + KW : QW + 2 * KW].reshape(row_count, KV_HEADS, HEAD_DIM)
    latent = projected_in[:, QW + 2 * KW :]
    queries = rotate(rms_norm(queries) * query_gain, cosine_part, sine_part)
    key_heads = rotate(rms_norm(key_heads) * key_gain, cosine_part, sine_part)
    value_heads = rms_norm(value_heads)
    return (queries, key_heads, value_heads, latent)


def join_piece(hidden_in, normed, attended, laurel_raw, gain_laurel, gain_attn, gain_ffin):
    joined = (
        hidden_in + rms_norm(attended) * gain_attn + normed + rms_norm(laurel_raw) * gain_laurel
    ) * INV_ROOT2
    return (joined, rms_norm(joined) * gain_ffin)


def gated_gelu(gate_pre, up_pre):
    return jax.nn.gelu(gate_pre, approximate=True) * up_pre


def add_branch(residual, branch, gain_out):
    return residual + rms_norm(branch) * gain_out


def dot(left_side, right_side):
    return jnp.dot(left_side, right_side, preferred_element_type=F32)


def dot_rows(left_side, right_side):
    return lax.dot_general(
        left_side, right_side, (((1,), (1,)), ((), ())), preferred_element_type=F32
    )


def dot_first(left_side, right_side):
    return lax.dot_general(
        left_side, right_side, (((0,), (0,)), ((), ())), preferred_element_type=F32
    )


def halves(value, core):
    left, right = value[..., :HALF], value[..., HALF:]
    return jnp.where(core == 0, left, right), jnp.where(core == 0, right, left)


def rejoin(own, other, core):
    return jnp.concatenate(
        [jnp.where(core == 0, own, other), jnp.where(core == 0, other, own)], axis=-1
    )


def rows_product(value, rows, start, stop, core):
    own, other = halves(value, core)
    return dot_rows(own, rows[0][start:stop]) + dot_rows(other, rows[1][start:stop])


def back_product(value, rows, start, stop, core):
    return rejoin(dot(value, rows[0][start:stop]), dot(value, rows[1][start:stop]), core)


def per_device(tokens, cotangent, block_ids, token_ids, attn_weight, ff_weight, gains, table):
    core = lax.axis_index("section")
    me = lax.axis_index("shard")
    n = lax.axis_size("shard")
    seq = tokens.shape[1]
    rows_dev = attn_weight.shape[1]
    units = ff_weight.shape[2]
    gains_dev = gains.shape[1]
    vocab_dev = table.shape[1]
    side = chip_dims(n)[2]
    plane = n // side

    def by_layer(mine, theirs):
        return (jnp.where(core == 0, mine, theirs), jnp.where(core == 0, theirs, mine))

    all_ids = lax.all_gather(token_ids.reshape(-1), "shard", axis=0, tiled=True)
    one_hot = (
        (all_ids - me * vocab_dev)[:, None] == jnp.arange(vocab_dev, dtype=jnp.int32)[None, :]
    ).astype(BF)
    looked_up = dot(one_hot, table[0]).astype(BF)
    looked_up = lax.psum_scatter(looked_up, "shard", scatter_dimension=0, tiled=True)
    looked_up = looked_up.reshape(2, seq, PLD)
    side_mine = jnp.where(core == 0, looked_up[0], looked_up[1])
    side_theirs = swap_cores(jnp.where(core == 0, looked_up[1], looked_up[0]))
    side_inputs = [value.astype(F32) for value in by_layer(side_mine, side_theirs)]

    own_half, other_half = halves(attn_weight[0], core)
    attn_blocks = by_layer(own_half, swap_cores(other_half))
    gain_blocks = by_layer(gains[0], swap_cores(gains[0]))
    gain_rows_block = jnp.zeros((8, HALF), BF)
    gain_rows_block = gain_rows_block.at[0, :gains_dev].set(gain_blocks[0])
    gain_rows_block = gain_rows_block.at[1, :gains_dev].set(gain_blocks[1])
    first = (rows_dev // 2 + 7) // 8 * 8
    second = rows_dev - first
    orders = (ZXY, ZYX)
    pieces = [
        (attn_blocks[0][:first], orders[0]),
        (jnp.concatenate([attn_blocks[0][first:], gain_rows_block], axis=0), orders[1]),
    ]
    found = gather_tree(pieces, n)
    row_buffers = [jnp.zeros((n, rows_dev, HALF), BF), jnp.zeros((n, rows_dev, HALF), BF)]
    gain_buffer = jnp.zeros((n, 8, HALF), BF)
    for p, (start, count) in enumerate(((0, first), (first, second))):
        for offset, block in found[p].items():
            source = source_index(me, n, orders[p], offset)
            where_to = (source, jnp.int32(start), jnp.int32(0))
            sent = swap_cores(block[:count])
            row_buffers[0] = lax.dynamic_update_slice(row_buffers[0], block[None, :count], where_to)
            row_buffers[1] = lax.dynamic_update_slice(row_buffers[1], sent[None], where_to)
            if p == 1:
                gain_buffer = lax.dynamic_update_slice(
                    gain_buffer, block[None, count:], (source, jnp.int32(0), jnp.int32(0))
                )
    rows_0 = [buffer.reshape(n * rows_dev, HALF) for buffer in row_buffers]
    rows_1_own = lax.all_gather(attn_blocks[1], "shard", axis=0, tiled=True)
    rows_1 = [rows_1_own, swap_cores(rows_1_own)]
    attn_rows = (rows_0, rows_1)
    layer_gains = [
        gain_buffer[:, layer, :gains_dev].reshape(n * gains_dev).astype(F32) for layer in range(2)
    ]

    ff_own = by_layer(ff_weight[0], swap_cores(ff_weight[0]))
    half_units = units // 2

    def ff_units(layer):
        mine = lax.dynamic_slice_in_dim(ff_own[layer], core * half_units, half_units, 1)
        parts = [ff_own[layer]]
        current = mine
        for _ in range(side - 1):
            current = hop(current, n, 2, 1)
            parts += [current, swap_cores(current)]
        return jnp.concatenate(parts, axis=1)

    ff_all = [ff_units(0), ff_units(1)]

    positions = me * seq + jnp.arange(seq, dtype=jnp.int32)
    cosine_part, sine_part = rope_tables(positions)
    head_split = partial(split_heads, cosine_part=cosine_part, sine_part=sine_part)
    key_offsets = offsets_of(n, ZXY)
    sources = jnp.stack([source_index(me, n, ZXY, offset) for offset in key_offsets])
    blocks = jnp.where(core == 0, block_ids[0], block_ids[1]).reshape(n, seq)
    key_blocks = jnp.take(blocks, sources, axis=0).reshape(-1)
    allowed = key_blocks[None, :] <= key_blocks[:seq, None]
    hidden_b = jnp.where(core == 0, tokens[0], tokens[1])

    def plane_gather(value):
        found = gather_tree([(value, ZY)], n, fence=False)[0]
        return jnp.concatenate([found[offset] for offset in offsets_of(n, ZY)], axis=0)

    def plane_scatter(value):
        terms = {
            offset: value[i * seq : (i + 1) * seq] for i, offset in enumerate(offsets_of(n, ZY))
        }
        return scatter_tree([(terms, ZY)], n)[0]

    def forward(layer, hidden_b):
        rows = attn_rows[layer]
        gain_flat = layer_gains[layer]
        gain_rows = gain_flat[: 6 * D].reshape(6, D)
        query_gain = gain_flat[6 * D : 6 * D + HEAD_DIM]
        key_gain = gain_flat[6 * D + HEAD_DIM :]
        hidden_in = hidden_b.astype(F32)
        normed = scaled_norm(hidden_in, gain_rows[0])
        normed_b = normed.astype(BF)
        projected_in = rows_product(normed_b, rows, 0, IN_ROWS, core)
        queries, key_heads, value_heads, latent = head_split(projected_in, query_gain, key_gain)
        queries_b = queries.astype(BF).reshape(seq, KV_HEADS, HEADS // KV_HEADS, HEAD_DIM)
        local = jnp.concatenate(
            [key_heads.reshape(seq, KW), value_heads.reshape(seq, KW)], axis=1
        ).astype(BF)
        found = gather_tree([(local, ZXY)], n, fence=False)[0]
        key_value = jnp.concatenate([found[offset] for offset in key_offsets], axis=0)
        keys_b = key_value[:, :KW].reshape(-1, KV_HEADS, HEAD_DIM)
        values_b = key_value[:, KW:].reshape(-1, KV_HEADS, HEAD_DIM)
        scores = (
            jnp.einsum("qkgd,jkd->kgqj", queries_b, keys_b, preferred_element_type=F32) * SCALE
        )
        scores = jnp.where(allowed, scores, MASKED)
        row_max = jnp.max(scores, axis=-1, keepdims=True)
        exponentials = jnp.exp(scores - row_max)
        probabilities = exponentials / jnp.sum(exponentials, axis=-1, keepdims=True)
        mixed_b = (
            jnp.einsum(
                "kgqj,jkd->qkgd", probabilities.astype(BF), values_b, preferred_element_type=F32
            )
            .reshape(seq, QW)
            .astype(BF)
        )
        attended = back_product(mixed_b, rows, OUT_START, LAUREL_START, core)
        latent_b = latent.astype(BF)
        laurel_raw = back_product(latent_b, rows, LAUREL_START, SIDE_START, core)
        joined, prenorm = join_piece(
            hidden_in, normed, attended, laurel_raw, gain_rows[1], gain_rows[2], gain_rows[3]
        )
        prenorm_all = plane_gather(prenorm.astype(BF))
        weights = ff_all[layer]
        gate = dot_rows(prenorm_all, weights[0])
        up = dot_rows(prenorm_all, weights[1])
        hidden_ff_b = gated_gelu(gate, up).astype(BF)
        down_out = plane_scatter(dot(hidden_ff_b, weights[2]))
        settled = add_branch(joined, down_out, gain_rows[4])
        settled_b = settled.astype(BF)
        side_gate = rows_product(settled_b, rows, IN_ROWS, OUT_START, core)
        gated_b = gated_gelu(side_gate, side_inputs[layer]).astype(BF)
        projected = back_product(gated_b, rows, SIDE_START, SIDE_START + PLD, core)
        layer_out_b = add_branch(settled, projected, gain_rows[5]).astype(BF)
        return layer_out_b, dict(
            hidden_in=hidden_in,
            normed=normed,
            normed_b=normed_b,
            projected_in=projected_in,
            queries_b=queries_b,
            keys_b=keys_b,
            values_b=values_b,
            probabilities=probabilities,
            mixed_b=mixed_b,
            attended=attended,
            latent_b=latent_b,
            laurel_raw=laurel_raw,
            joined=joined,
            prenorm_all=prenorm_all,
            gate=gate,
            up=up,
            hidden_ff_b=hidden_ff_b,
            down_out=down_out,
            settled=settled,
            settled_b=settled_b,
            side_gate=side_gate,
            gated_b=gated_b,
            projected=projected,
        )

    def both(left, right):
        own, other = halves(right, core)
        lefts = jnp.concatenate([left, swap_cores(left)], axis=0)
        rights = jnp.concatenate([own, swap_cores(other)], axis=0)
        return dot_first(lefts, rights).astype(BF)

    def backward(layer, kept, grad_out_b):
        rows = attn_rows[layer]
        weights = ff_all[layer]
        gain_flat = layer_gains[layer]
        gain_rows = gain_flat[: 6 * D].reshape(6, D)
        query_gain = gain_flat[6 * D : 6 * D + HEAD_DIM]
        key_gain = gain_flat[6 * D + HEAD_DIM :]
        grad_out = grad_out_b.astype(F32)
        grad_settled, grad_projected, grad_gain5 = jax.vjp(
            add_branch, kept["settled"], kept["projected"], gain_rows[5]
        )[1](grad_out)
        grad_projected_b = grad_projected.astype(BF)
        grad_gated = rows_product(grad_projected_b, rows, SIDE_START, SIDE_START + PLD, core)
        grad_side_gate, grad_side = jax.vjp(gated_gelu, kept["side_gate"], side_inputs[layer])[1](
            grad_gated
        )
        grad_side_gate_b = grad_side_gate.astype(BF)
        grad_settled = grad_settled + back_product(
            grad_side_gate_b, rows, IN_ROWS, OUT_START, core
        )
        grad_joined, grad_down, grad_gain4 = jax.vjp(
            add_branch, kept["joined"], kept["down_out"], gain_rows[4]
        )[1](grad_settled)
        grad_down_all = plane_gather(grad_down.astype(BF))
        grad_hidden_ff = dot_rows(grad_down_all, weights[2])
        grad_gate, grad_up = jax.vjp(gated_gelu, kept["gate"], kept["up"])[1](grad_hidden_ff)
        grad_gate_b, grad_up_b = grad_gate.astype(BF), grad_up.astype(BF)
        grad_prenorm = plane_scatter(dot(grad_gate_b, weights[0]) + dot(grad_up_b, weights[1]))
        ff_term = jnp.stack(
            [
                dot_first(grad_gate_b, kept["prenorm_all"]).astype(BF),
                dot_first(grad_up_b, kept["prenorm_all"]).astype(BF),
                dot_first(kept["hidden_ff_b"], grad_down_all).astype(BF),
            ]
        )
        passed = None
        for steps in range(side - 1, 0, -1):
            start = units + 2 * (steps - 1) * half_units
            near = ff_term[:, start : start + half_units].astype(F32)
            far = swap_cores(ff_term[:, start + half_units : start + 2 * half_units])
            term = near + far.astype(F32)
            if passed is not None:
                term = term + passed.astype(F32)
            passed = hop(term.astype(BF), n, 2, -1)
        ff_sum = (ff_term[:, :units], passed)
        join_pull = jax.vjp(
            join_piece,
            kept["hidden_in"],
            kept["normed"],
            kept["attended"],
            kept["laurel_raw"],
            gain_rows[1],
            gain_rows[2],
            gain_rows[3],
        )[1]
        grad_hidden, grad_normed, grad_attended, grad_laurel, grad_gain1, grad_gain2, grad_gain3 = (
            join_pull((grad_joined, grad_prenorm))
        )
        grad_attended_b = grad_attended.astype(BF)
        grad_laurel_b = grad_laurel.astype(BF)
        grad_mixed_b = rows_product(grad_attended_b, rows, OUT_START, LAUREL_START, core).astype(BF)
        grad_latent = rows_product(grad_laurel_b, rows, LAUREL_START, SIDE_START, core)
        grad_mixed_heads = grad_mixed_b.reshape(seq, KV_HEADS, HEADS // KV_HEADS, HEAD_DIM)
        probabilities = kept["probabilities"]
        grad_probs = jnp.einsum(
            "qkgd,jkd->kgqj", grad_mixed_heads, kept["values_b"], preferred_element_type=F32
        )
        row_dot = jnp.sum(grad_probs * probabilities, axis=-1, keepdims=True)
        grad_scores_b = (probabilities * (grad_probs - row_dot)).astype(BF)
        grad_queries = (
            jnp.einsum("kgqj,jkd->qkgd", grad_scores_b, kept["keys_b"], preferred_element_type=F32)
            * SCALE
        )
        grad_keys_all = (
            jnp.einsum(
                "kgqj,qkgd->jkd", grad_scores_b, kept["queries_b"], preferred_element_type=F32
            )
            * SCALE
        )
        grad_values_all = jnp.einsum(
            "kgqj,qkgd->jkd",
            probabilities.astype(BF),
            grad_mixed_heads,
            preferred_element_type=F32,
        )
        grad_key_value = jnp.concatenate(
            [grad_keys_all.reshape(-1, KW), grad_values_all.reshape(-1, KW)], axis=1
        )
        terms = {
            offset: grad_key_value[i * seq : (i + 1) * seq] for i, offset in enumerate(key_offsets)
        }
        grad_local = scatter_tree([(terms, ZXY)], n)[0]
        head_pull = jax.vjp(head_split, kept["projected_in"], query_gain, key_gain)[1]
        grad_projected_in, grad_query_gain, grad_key_gain = head_pull(
            (
                grad_queries.reshape(seq, HEADS, HEAD_DIM),
                grad_local[:, :KW].reshape(seq, KV_HEADS, HEAD_DIM),
                grad_local[:, KW:].reshape(seq, KV_HEADS, HEAD_DIM),
                grad_latent,
            )
        )
        grad_projected_in_b = grad_projected_in.astype(BF)
        grad_normed = grad_normed + back_product(grad_projected_in_b, rows, 0, IN_ROWS, core)
        grad_front, grad_gain0 = jax.vjp(scaled_norm, kept["hidden_in"], gain_rows[0])[1](
            grad_normed
        )
        grad_hidden_b = (grad_hidden + grad_front).astype(BF)
        gain_vec = jnp.concatenate(
            [
                grad_gain0,
                grad_gain1,
                grad_gain2,
                grad_gain3,
                grad_gain4,
                grad_gain5,
                grad_query_gain,
                grad_key_gain,
            ]
        )
        attn_term = jnp.concatenate(
            [
                both(grad_projected_in_b, kept["normed_b"]),
                both(grad_side_gate_b, kept["settled_b"]),
                both(kept["mixed_b"], grad_attended_b),
                both(kept["latent_b"], grad_laurel_b),
                both(kept["gated_b"], grad_projected_b),
            ],
            axis=0,
        )
        return grad_hidden_b, attn_term, ff_sum, gain_vec, grad_side.astype(BF)

    out_0, kept_0 = forward(0, hidden_b)
    out_1, kept_1 = forward(1, out_0)
    top = jnp.where(core == 0, cotangent[0], cotangent[1])
    grad_1, attn_term_1, ff_sum_1, gain_vec_1, grad_side_1 = backward(1, kept_1, top)
    attn_sum_1 = lax.psum_scatter(attn_term_1, "shard", scatter_dimension=0, tiled=True)
    grad_0, attn_term_0, ff_sum_0, gain_vec_0, grad_side_0 = backward(0, kept_0, grad_1)

    attn_terms = attn_term_0.reshape(n, rows_dev, HALF)
    gain_terms = jnp.stack(
        [gain_vec_0.reshape(n, gains_dev), gain_vec_1.reshape(n, gains_dev)], axis=1
    )
    gain_terms = jnp.pad(gain_terms, ((0, 0), (0, 6), (0, HALF - gains_dev))).astype(BF)
    piece_terms = [{}, {}]
    for p in range(2):
        for offset in offsets_of(n, orders[p]):
            source = source_index(me, n, orders[p], offset)
            block = lax.dynamic_index_in_dim(attn_terms, source, 0, keepdims=False)
            if p == 0:
                piece_terms[0][offset] = block[:first]
            else:
                gain_block = lax.dynamic_index_in_dim(gain_terms, source, 0, keepdims=False)
                piece_terms[1][offset] = jnp.concatenate([block[first:], gain_block], axis=0)
    sum_first, sum_second = scatter_tree(
        [(piece_terms[0], orders[0]), (piece_terms[1], orders[1])], n
    )
    attn_sum_0 = jnp.concatenate([sum_first, sum_second[:second]], axis=0)
    attn_sum_1 = attn_sum_1.astype(F32)
    attn_keep = jnp.where(core == 0, attn_sum_0, attn_sum_1)
    attn_other = swap_cores(jnp.where(core == 0, attn_sum_1, attn_sum_0))
    attn_grad = rejoin(attn_keep, attn_other, core)
    gain_sums = sum_second[second : second + 2, :gains_dev]
    gain_grad = jnp.where(core == 0, gain_sums[0], gain_sums[1]) + swap_cores(
        jnp.where(core == 0, gain_sums[1], gain_sums[0])
    )

    def whole_ff(ff_sum):
        base, passed = ff_sum
        zeros = jnp.zeros((3, units - half_units, D), BF)
        placed = jnp.where(
            core == 0,
            jnp.concatenate([passed, zeros], axis=1),
            jnp.concatenate([zeros, passed], axis=1),
        )
        return base.astype(F32) + placed.astype(F32)

    whole_0, whole_1 = whole_ff(ff_sum_0), whole_ff(ff_sum_1)
    ff_grad = jnp.where(core == 0, whole_0, whole_1) + swap_cores(
        jnp.where(core == 0, whole_1, whole_0).astype(BF)
    ).astype(F32)

    side_keep = jnp.where(core == 0, grad_side_0, grad_side_1)
    side_other = swap_cores(jnp.where(core == 0, grad_side_1, grad_side_0))
    side_both = jnp.concatenate(
        [jnp.where(core == 0, side_keep, side_other), jnp.where(core == 0, side_other, side_keep)],
        axis=0,
    )
    side_all = lax.all_gather(side_both, "shard", axis=0, tiled=True)
    table_grad = dot_first(one_hot, side_all)

    def outputs_of(value_0, value_1):
        keep = jnp.where(core == 0, value_0, value_1)
        other = swap_cores(jnp.where(core == 0, value_1, value_0))
        return jnp.stack([jnp.where(core == 0, keep, other), jnp.where(core == 0, other, keep)])

    return (
        outputs_of(out_0, out_1)[None],
        outputs_of(grad_0, grad_1)[None],
        attn_grad[None],
        ff_grad[None],
        gain_grad[None],
        table_grad[None],
    )


def solution(mesh):
    placed = (
        P(None, "shard", None),
        P(None, "shard", None),
        P(),
        P(None, "shard"),
        P("section", "shard", None),
        P("section", None, "shard", None),
        P("section", "shard"),
        P("section", "shard", None),
    )
    return jax.shard_map(
        per_device,
        mesh=mesh,
        in_specs=placed,
        out_specs=(
            P("section", None, "shard", None),
            P("section", None, "shard", None),
            P("section", "shard", None),
            P("section", None, "shard", None),
            P("section", "shard"),
            P("section", "shard", None),
        ),
        check_vma=False,
    )
```

```python
import itertools
import math
from functools import partial

import jax
import jax.numpy as jnp
from jax import lax
from jax.sharding import PartitionSpec as P

D = 2048
HEADS = 8
KV_HEADS = 2
HEAD_DIM = 256
RANK = 64
PLD = 256
HALF = D // 2
QW = HEADS * HEAD_DIM
KW = KV_HEADS * HEAD_DIM
IN_ROWS = QW + 2 * KW + RANK
OUT_START = IN_ROWS + PLD
LAUREL_START = OUT_START + QW
SIDE_START = LAUREL_START + RANK

EPS = 1e-06
ROPE_BASE = 10000.0
INV_ROOT2 = 0.7071067811865476
MASKED = -1e30
SCALE = HEAD_DIM ** (-0.5)
BF = jnp.bfloat16
F32 = jnp.float32

ALL_CHIPS = ((0, 2, 1), (0, 1, 2))
PLANE = ((0, 1), (0, 1))


def tie(*values):
    return lax.optimization_barrier(values)


def chip_dims(n):
    side = math.isqrt(n // 4)
    return (4, side, side)


def chip_strides(n):
    sizes = chip_dims(n)
    return (sizes[1] * sizes[2], sizes[2], 1)


def hop(value, n, dims, step):
    sizes, strides = chip_dims(n), chip_strides(n)
    pairs = []
    for core, dim in enumerate(dims):
        for i in range(n):
            place = (i // strides[dim]) % sizes[dim]
            target = i + ((place + step) % sizes[dim] - place) * strides[dim]
            pairs.append((core * n + i, core * n + target))
    return lax.ppermute(value, ("section", "shard"), pairs)


def swap_cores(value):
    return lax.ppermute(value, "section", [(0, 1), (1, 0)])


def offsets_of(n, orders):
    sizes = chip_dims(n)
    return list(itertools.product(*[range(sizes[d]) for d in orders[0]]))


def tree(n, orders):
    rounds = {}
    for offset in offsets_of(n, orders):
        if sum(offset) > 0:
            last = max(i for i, steps in enumerate(offset) if steps > 0)
            parent = tuple(steps - (i == last) for i, steps in enumerate(offset))
            edge = (offset, parent, (orders[0][last], orders[1][last]))
            rounds.setdefault(sum(offset), []).append(edge)
    return [rounds[number] for number in sorted(rounds)]


def source_index(me, core, n, orders, offset):
    sizes, strides = chip_dims(n), chip_strides(n)
    found = []
    for order in orders:
        index = me
        for dim, steps in zip(order, offset):
            place = (me // strides[dim]) % sizes[dim]
            index = index + ((place - steps) % sizes[dim] - place) * strides[dim]
        found.append(index)
    return jnp.where(core == 0, found[0], found[1])


def gather_tree(block, n, orders):
    found = {(0,) * len(orders[0]): block}
    for edges in tree(n, orders):
        for offset, parent, dims in edges:
            found[offset] = hop(found[parent], n, dims, 1)
    return found


def scatter_steps(terms, n, orders, sums):
    totals = dict(terms)
    for edges in reversed(tree(n, orders)):
        sent = [hop(totals[offset].astype(BF), n, dims, -1) for offset, _, dims in edges]
        sent, _ = yield sent
        for (_, parent, _), value in zip(edges, sent):
            totals[parent] = totals[parent].astype(F32) + value.astype(F32)
    sums.append(totals[(0,) * len(orders[0])])


def run(job):
    sent = next(job)
    while True:
        try:
            sent = job.send((sent, None))
        except StopIteration:
            return


def scatter_tree(terms, n, orders):
    sums = []
    run(scatter_steps(terms, n, orders, sums))
    return sums[0]


class Background:
    def __init__(self):
        self.jobs = []

    def add(self, job):
        self.jobs.append((job, next(job)))

    def stage(self, *values):
        values, flying = lax.optimization_barrier((values, [sent for _, sent in self.jobs]))
        going = []
        for (job, _), sent in zip(self.jobs, flying):
            try:
                going.append((job, job.send((sent, values[0]))))
            except StopIteration:
                pass
        self.jobs = going
        return values

    def drain(self):
        while self.jobs:
            going = []
            for job, sent in self.jobs:
                try:
                    going.append((job, job.send((sent, None))))
                except StopIteration:
                    pass
            self.jobs = going


def after(value, anchor):
    return value if anchor is None else tie(value, anchor)[0]


def gather_small(value, me, n):
    step = 1
    while step < n:
        other = lax.ppermute(value, "shard", [(i, i ^ step) for i in range(n)])
        lower = (me // step) % 2 == 0
        value = jnp.where(
            lower,
            jnp.concatenate([value, other], axis=0),
            jnp.concatenate([other, value], axis=0),
        )
        step *= 2
    return value


def rms_norm(values):
    return values * lax.rsqrt(jnp.mean(values * values, axis=-1, keepdims=True) + EPS)


def scaled_norm(values, gain_vec):
    return rms_norm(values) * gain_vec


def rope_tables(positions):
    half_width = HEAD_DIM // 2
    frequency = ROPE_BASE ** (-jnp.arange(half_width, dtype=F32) * (2.0 / HEAD_DIM))
    angles = positions.astype(F32)[:, None] * frequency[None, :]
    return (jnp.cos(angles), jnp.sin(angles))


def rotate(vectors, cosine_part, sine_part):
    half_width = vectors.shape[-1] // 2
    first_half = vectors[..., :half_width]
    second_half = vectors[..., half_width:]
    cosine_rows = cosine_part[:, None, :]
    sine_rows = sine_part[:, None, :]
    return jnp.concatenate(
        [
            first_half * cosine_rows - second_half * sine_rows,
            second_half * cosine_rows + first_half * sine_rows,
        ],
        axis=-1,
    )


def query_heads(projected, query_gain, cosine_part, sine_part):
    heads = projected.reshape(projected.shape[0], HEADS, HEAD_DIM)
    return rotate(rms_norm(heads) * query_gain, cosine_part, sine_part)


def key_value_heads(projected, key_gain, cosine_part, sine_part):
    row_count = projected.shape[0]
    key_heads = projected[:, :KW].reshape(row_count, KV_HEADS, HEAD_DIM)
    value_heads = projected[:, KW:].reshape(row_count, KV_HEADS, HEAD_DIM)
    key_heads = rotate(rms_norm(key_heads) * key_gain, cosine_part, sine_part)
    return jnp.concatenate(
        [key_heads.reshape(row_count, KW), rms_norm(value_heads).reshape(row_count, KW)], axis=1
    )


def join_piece(hidden_in, normed, attended, laurel_raw, gain_laurel, gain_attn, gain_ffin):
    joined = (
        hidden_in + rms_norm(attended) * gain_attn + normed + rms_norm(laurel_raw) * gain_laurel
    ) * INV_ROOT2
    return (joined, rms_norm(joined) * gain_ffin)


def gated_gelu(gate_pre, up_pre):
    return jax.nn.gelu(gate_pre, approximate=True) * up_pre


def add_branch(residual, branch, gain_out):
    return residual + rms_norm(branch) * gain_out


def dot(left_side, right_side):
    return jnp.dot(left_side, right_side, preferred_element_type=F32)


def dot_rows(left_side, right_side):
    return lax.dot_general(
        left_side, right_side, (((1,), (1,)), ((), ())), preferred_element_type=F32
    )


def dot_first(left_side, right_side):
    return lax.dot_general(
        left_side, right_side, (((0,), (0,)), ((), ())), preferred_element_type=F32
    )


def halves(value, core):
    left, right = value[..., :HALF], value[..., HALF:]
    return jnp.where(core == 0, left, right), jnp.where(core == 0, right, left)


def rejoin(own, other, core):
    return jnp.concatenate(
        [jnp.where(core == 0, own, other), jnp.where(core == 0, other, own)], axis=-1
    )


def rows_product(value, rows, start, stop, core):
    own, other = halves(value, core)
    return dot_rows(own, rows[0][start:stop]) + dot_rows(other, rows[1][start:stop])


def back_product(value, rows, start, stop, core):
    return rejoin(dot(value, rows[0][start:stop]), dot(value, rows[1][start:stop]), core)


def per_device(tokens, cotangent, block_ids, token_ids, attn_weight, ff_weight, gains, table):
    core = lax.axis_index("section")
    me = lax.axis_index("shard")
    n = lax.axis_size("shard")
    seq = tokens.shape[1]
    rows_dev = attn_weight.shape[1]
    units = ff_weight.shape[2]
    half_units = units // 2
    gains_dev = gains.shape[1]
    vocab_dev = table.shape[1]
    side = chip_dims(n)[2]
    background = Background()

    def pick(for_0, for_1):
        return jnp.where(core == 0, for_0, for_1)

    def by_layer(mine, theirs):
        return (pick(mine, theirs), pick(theirs, mine))

    gain_pair = by_layer(gains[0].astype(F32), swap_cores(gains[0]).astype(F32))
    small = jnp.concatenate([gain_pair[0], gain_pair[1], token_ids.reshape(-1).astype(F32)])
    small_all = gather_small(small[None], me, n)
    layer_gains = [
        small_all[:, layer * gains_dev : (layer + 1) * gains_dev].reshape(n * gains_dev)
        for layer in range(2)
    ]
    all_ids = small_all[:, 2 * gains_dev :].astype(jnp.int32).reshape(-1)

    one_hot = (
        (all_ids - me * vocab_dev)[:, None] == jnp.arange(vocab_dev, dtype=jnp.int32)[None, :]
    ).astype(BF)
    looked_up = dot(one_hot, table[0]).astype(BF)
    looked_up = lax.psum_scatter(looked_up, "shard", scatter_dimension=0, tiled=True)
    looked_up = looked_up.reshape(2, seq, PLD)
    side_theirs = swap_cores(pick(looked_up[1], looked_up[0]))
    side_inputs = [
        value.astype(F32) for value in by_layer(pick(looked_up[0], looked_up[1]), side_theirs)
    ]

    own_half, other_half = halves(attn_weight[0], core)
    attn_blocks = by_layer(own_half, swap_cores(other_half))
    ff_own = by_layer(ff_weight[0], swap_cores(ff_weight[0]))
    ff_half = [lax.dynamic_slice_in_dim(own, core * half_units, half_units, 1) for own in ff_own]
    buffers = [jnp.zeros((n, rows_dev, HALF), BF), jnp.zeros((n, rows_dev, HALF), BF)]

    def store_blocks(buffers, fresh):
        for offset, block in fresh.items():
            sources = [source_index(me, c, n, ALL_CHIPS, offset) for c in (core, 1 - core)]
            buffers = [
                lax.dynamic_update_slice(
                    buffer, value[None], (source, jnp.int32(0), jnp.int32(0))
                )
                for buffer, value, source in zip(buffers, (block, swap_cores(block)), sources)
            ]
        return buffers

    fresh = {(0, 0, 0): attn_blocks[0]}
    held = dict(fresh)
    for edges in tree(n, ALL_CHIPS):
        arriving = {offset: hop(held[parent], n, dims, 1) for offset, parent, dims in edges}
        buffers = store_blocks(buffers, fresh)
        fresh, held, buffers = tie(arriving, held, buffers)
        held.update(fresh)
    last_block = fresh[max(fresh)]
    buffers = store_blocks(buffers, fresh)
    rows_0 = [buffer.reshape(n * rows_dev, HALF) for buffer in buffers]
    next_block, last_block, ff_own, ff_half, _ = tie(
        attn_blocks[1], last_block, ff_own, ff_half, looked_up
    )
    rows_1_own = lax.all_gather(next_block, "shard", axis=0, tiled=True)
    rows_1 = [rows_1_own, swap_cores(rows_1_own)]
    attn_rows = (rows_0, rows_1)

    positions = me * seq + jnp.arange(seq, dtype=jnp.int32)
    cosine_part, sine_part = rope_tables(positions)
    query_split = partial(query_heads, cosine_part=cosine_part, sine_part=sine_part)
    key_value_split = partial(key_value_heads, cosine_part=cosine_part, sine_part=sine_part)
    key_offsets = offsets_of(n, ALL_CHIPS)
    plane_offsets = offsets_of(n, PLANE)
    sources = jnp.stack([source_index(me, core, n, ALL_CHIPS, offset) for offset in key_offsets])
    blocks = pick(block_ids[0], block_ids[1]).reshape(n, seq)
    key_blocks = jnp.take(blocks, sources, axis=0).reshape(-1)
    allowed = key_blocks[None, :] <= key_blocks[:seq, None]
    hidden_b = pick(tokens[0], tokens[1])

    def near_units(layer, anchor, near):
        for which in range(3):
            current = after(ff_half[layer][which], anchor)
            parts = []
            for _ in range(side - 1):
                (current,), anchor = yield [hop(current, n, (2, 2), 1)]
                parts.append(current)
            near.append(parts)

    def plane_gather(value):
        found = gather_tree(value, n, PLANE)
        return jnp.concatenate([found[offset] for offset in plane_offsets], axis=0)

    def plane_scatter(value):
        terms = {o: value[i * seq : (i + 1) * seq] for i, o in enumerate(plane_offsets)}
        return scatter_tree(terms, n, PLANE)

    def split_gains(layer):
        flat = layer_gains[layer]
        return flat[: 6 * D].reshape(6, D), flat[6 * D : 6 * D + HEAD_DIM], flat[6 * D + HEAD_DIM :]

    def forward(layer, hidden_b, near):
        rows = attn_rows[layer]
        gain_rows, query_gain, key_gain = split_gains(layer)
        hidden_in = hidden_b.astype(F32)
        normed = scaled_norm(hidden_in, gain_rows[0])
        normed_b = normed.astype(BF)
        projected_kv = rows_product(normed_b, rows, QW, QW + 2 * KW, core)
        local = key_value_split(projected_kv, key_gain).astype(BF)
        (local,) = background.stage(local)
        found = gather_tree(local, n, ALL_CHIPS)
        projected_q = rows_product(normed_b, rows, 0, QW, core)
        queries_b = query_split(projected_q, query_gain).astype(BF)
        queries_b = queries_b.reshape(seq, KV_HEADS, HEADS // KV_HEADS, HEAD_DIM)
        latent_b = rows_product(normed_b, rows, QW + 2 * KW, IN_ROWS, core).astype(BF)
        laurel_raw = back_product(latent_b, rows, LAUREL_START, SIDE_START, core)
        key_value = jnp.concatenate([found[offset] for offset in key_offsets], axis=0)
        key_value, queries_b, laurel_raw = background.stage(key_value, queries_b, laurel_raw)
        keys_b = key_value[:, :KW].reshape(-1, KV_HEADS, HEAD_DIM)
        values_b = key_value[:, KW:].reshape(-1, KV_HEADS, HEAD_DIM)
        scores = (
            jnp.einsum("qkgd,jkd->kgqj", queries_b, keys_b, preferred_element_type=F32) * SCALE
        )
        scores = jnp.where(allowed, scores, MASKED)
        row_max = jnp.max(scores, axis=-1, keepdims=True)
        exponentials = jnp.exp(scores - row_max)
        probabilities = exponentials / jnp.sum(exponentials, axis=-1, keepdims=True)
        mixed_b = (
            jnp.einsum(
                "kgqj,jkd->qkgd", probabilities.astype(BF), values_b, preferred_element_type=F32
            )
            .reshape(seq, QW)
            .astype(BF)
        )
        attended = back_product(mixed_b, rows, OUT_START, LAUREL_START, core)
        joined, prenorm = join_piece(
            hidden_in, normed, attended, laurel_raw, gain_rows[1], gain_rows[2], gain_rows[3]
        )
        (prenorm_b,) = background.stage(prenorm.astype(BF))
        prenorm_all = plane_gather(prenorm_b)
        (prenorm_all,) = background.stage(prenorm_all)
        while len(near) < 3:
            (prenorm_all,) = background.stage(prenorm_all)
        weights = [
            [ff_own[layer][which]]
            + [part for through in near[which] for part in (through, swap_cores(through))]
            for which in range(3)
        ]
        gate = [dot_rows(prenorm_all, part) for part in weights[0]]
        up = [dot_rows(prenorm_all, part) for part in weights[1]]
        hidden_ff_b = [gated_gelu(g, u).astype(BF) for g, u in zip(gate, up)]
        down_out = plane_scatter(sum(dot(h, part) for h, part in zip(hidden_ff_b, weights[2])))
        (down_out,) = background.stage(down_out)
        settled = add_branch(joined, down_out, gain_rows[4])
        settled_b = settled.astype(BF)
        side_gate = rows_product(settled_b, rows, IN_ROWS, OUT_START, core)
        gated_b = gated_gelu(side_gate, side_inputs[layer]).astype(BF)
        projected = back_product(gated_b, rows, SIDE_START, SIDE_START + PLD, core)
        layer_out_b = add_branch(settled, projected, gain_rows[5]).astype(BF)
        return layer_out_b, dict(
            hidden_in=hidden_in,
            normed=normed,
            normed_b=normed_b,
            projected_q=projected_q,
            projected_kv=projected_kv,
            weights=weights,
            queries_b=queries_b,
            keys_b=keys_b,
            values_b=values_b,
            probabilities=probabilities,
            mixed_b=mixed_b,
            attended=attended,
            latent_b=latent_b,
            laurel_raw=laurel_raw,
            joined=joined,
            prenorm_all=prenorm_all,
            gate=gate,
            up=up,
            hidden_ff_b=hidden_ff_b,
            down_out=down_out,
            settled=settled,
            settled_b=settled_b,
            side_gate=side_gate,
            gated_b=gated_b,
            projected=projected,
        )

    def early_products(pairs):
        lefts = jnp.concatenate([left for left, _ in pairs], axis=1)
        lefts = jnp.concatenate([lefts, swap_cores(lefts)], axis=0)
        own, other = halves(jnp.stack([right for _, right in pairs]), core)
        rights = jnp.concatenate([own, swap_cores(other)], axis=1)
        terms = [jnp.zeros((IN_ROWS - upper_rows, HALF), BF)]
        start = 0
        for i, (left, _) in enumerate(pairs):
            stop = start + left.shape[1]
            terms.append(dot_first(lefts[:, start:stop], rights[i]).astype(BF))
            start = stop
        return jnp.concatenate(terms, axis=0)

    first = (rows_dev // 2 + 7) // 8 * 8
    upper_rows = n // 2 * rows_dev

    def early_rows(term, result):
        shaped = term.reshape(n // 2, rows_dev, HALF)
        upper = me >= n // 2
        pieces = {}
        for offset in key_offsets:
            target = source_index(me, core, n, ALL_CHIPS, offset)
            place = (target % (n // 2), jnp.where(target >= n // 2, 0, rows_dev - first), 0)
            pieces[offset] = lax.dynamic_slice(shaped, place, (1, first, HALF))[0]
        sums = []
        yield from scatter_steps(pieces, n, ALL_CHIPS, sums)
        mine = sums[0].astype(BF)
        sent = lax.ppermute(mine, "shard", [(i, i + n // 2) for i in range(n // 2)])
        (sent,), _ = yield [sent]
        whole = jnp.concatenate([mine, sent[2 * first - rows_dev :]], axis=0).astype(F32)
        result.append(jnp.where(upper, whole, 0.0))

    def backward(layer, kept, grad_out_b, passed, early, due):
        rows = attn_rows[layer]
        weights = kept["weights"]
        gain_rows, query_gain, key_gain = split_gains(layer)
        grad_out = grad_out_b.astype(F32)
        grad_settled, grad_projected, grad_gain5 = jax.vjp(
            add_branch, kept["settled"], kept["projected"], gain_rows[5]
        )[1](grad_out)
        grad_projected_b = grad_projected.astype(BF)
        grad_gated = rows_product(grad_projected_b, rows, SIDE_START, SIDE_START + PLD, core)
        grad_side_gate, grad_side = jax.vjp(gated_gelu, kept["side_gate"], side_inputs[layer])[1](
            grad_gated
        )
        grad_side_gate_b = grad_side_gate.astype(BF)
        grad_settled = grad_settled + back_product(
            grad_side_gate_b, rows, IN_ROWS, OUT_START, core
        )
        grad_joined, grad_down, grad_gain4 = jax.vjp(
            add_branch, kept["joined"], kept["down_out"], gain_rows[4]
        )[1](grad_settled)
        due[0].append(grad_side.astype(BF))
        (grad_down_b,) = background.stage(grad_down.astype(BF))
        grad_down_all = plane_gather(grad_down_b)
        (grad_down_all,) = background.stage(grad_down_all)
        grad_hidden_ff = [dot_rows(grad_down_all, part) for part in weights[2]]
        grad_gate_up = [
            jax.vjp(gated_gelu, g, u)[1](grad)
            for g, u, grad in zip(kept["gate"], kept["up"], grad_hidden_ff)
        ]
        grad_gate_b = [pair[0].astype(BF) for pair in grad_gate_up]
        grad_up_b = [pair[1].astype(BF) for pair in grad_gate_up]
        grad_prenorm = sum(
            dot(g, wg) + dot(u, wu)
            for g, u, wg, wu in zip(grad_gate_b, grad_up_b, weights[0], weights[1])
        )
        grad_prenorm, grad_gate_b, grad_up_b = tie(grad_prenorm, grad_gate_b, grad_up_b)
        grad_prenorm = plane_scatter(grad_prenorm)
        ff_terms = [
            [dot_first(g, kept["prenorm_all"]).astype(BF) for g in grad_gate_b],
            [dot_first(u, kept["prenorm_all"]).astype(BF) for u in grad_up_b],
            [dot_first(h, grad_down_all).astype(BF) for h in kept["hidden_ff_b"]],
        ]
        ff_base = jnp.stack([terms[0] for terms in ff_terms])
        pair_sums = [
            [
                (terms[1 + 2 * i].astype(F32) + swap_cores(terms[2 + 2 * i]).astype(F32)).astype(BF)
                for i in range(side - 1)
            ]
            for terms in ff_terms
        ]
        grad_prenorm, pair_sums, ff_base = background.stage(grad_prenorm, pair_sums, ff_base)

        def pass_back():
            anchor = None
            for which in range(3):
                carried = None
                for steps in range(side - 1, 0, -1):
                    term = after(pair_sums[which][steps - 1], anchor)
                    if carried is not None:
                        term = (term.astype(F32) + carried.astype(F32)).astype(BF)
                    (carried,), anchor = yield [hop(term, n, (2, 2), -1)]
                passed.append(carried)

        background.add(pass_back())
        join_pull = jax.vjp(
            join_piece,
            kept["hidden_in"],
            kept["normed"],
            kept["attended"],
            kept["laurel_raw"],
            gain_rows[1],
            gain_rows[2],
            gain_rows[3],
        )[1]
        grad_hidden, grad_normed, grad_attended, grad_laurel, grad_gain1, grad_gain2, grad_gain3 = (
            join_pull((grad_joined, grad_prenorm))
        )
        grad_attended_b = grad_attended.astype(BF)
        grad_laurel_b = grad_laurel.astype(BF)
        grad_mixed_b = rows_product(grad_attended_b, rows, OUT_START, LAUREL_START, core).astype(BF)
        grad_latent = rows_product(grad_laurel_b, rows, LAUREL_START, SIDE_START, core)
        grad_mixed_heads = grad_mixed_b.reshape(seq, KV_HEADS, HEADS // KV_HEADS, HEAD_DIM)
        probabilities = kept["probabilities"]
        grad_probs = jnp.einsum(
            "qkgd,jkd->kgqj", grad_mixed_heads, kept["values_b"], preferred_element_type=F32
        )
        row_dot = jnp.sum(grad_probs * probabilities, axis=-1, keepdims=True)
        grad_scores_b = (probabilities * (grad_probs - row_dot)).astype(BF)
        grad_keys_all = (
            jnp.einsum(
                "kgqj,qkgd->jkd", grad_scores_b, kept["queries_b"], preferred_element_type=F32
            )
            * SCALE
        )
        grad_values_all = jnp.einsum(
            "kgqj,qkgd->jkd",
            probabilities.astype(BF),
            grad_mixed_heads,
            preferred_element_type=F32,
        )
        grad_key_value = jnp.concatenate(
            [grad_keys_all.reshape(-1, KW), grad_values_all.reshape(-1, KW)], axis=1
        ).astype(BF)
        early_pairs = (
            (grad_side_gate_b, kept["settled_b"]),
            (kept["mixed_b"], grad_attended_b),
            (kept["latent_b"], grad_laurel_b),
            (kept["gated_b"], grad_projected_b),
        )
        work = due[1]() if callable(due[1]) else due[1]
        grad_key_value, early_pairs, work = background.stage(grad_key_value, early_pairs, work)
        early_term = early_products(early_pairs)
        due[1] = due[2](work)
        terms = {o: grad_key_value[i * seq : (i + 1) * seq] for i, o in enumerate(key_offsets)}
        grad_local = scatter_tree(terms, n, ALL_CHIPS)
        grad_queries = (
            jnp.einsum("kgqj,jkd->qkgd", grad_scores_b, kept["keys_b"], preferred_element_type=F32)
            * SCALE
        )
        grad_projected_q, grad_query_gain = jax.vjp(query_split, kept["projected_q"], query_gain)[
            1
        ](grad_queries.reshape(seq, HEADS, HEAD_DIM))
        grad_q_b, grad_z_b = grad_projected_q.astype(BF), grad_latent.astype(BF)
        grad_normed = (
            grad_normed
            + back_product(grad_q_b, rows, 0, QW, core)
            + back_product(grad_z_b, rows, QW + 2 * KW, IN_ROWS, core)
        )
        grad_local, grad_normed, early_term, due[1] = background.stage(
            grad_local, grad_normed, early_term, due[1]
        )
        if layer == 1:
            background.add(early_rows(early_term, early))
        else:
            early.append(early_term)
        grad_projected_kv, grad_key_gain = jax.vjp(
            key_value_split, kept["projected_kv"], key_gain
        )[1](grad_local)
        grad_kv_b = grad_projected_kv.astype(BF)
        grad_normed = grad_normed + back_product(grad_kv_b, rows, QW, QW + 2 * KW, core)
        grad_front, grad_gain0 = jax.vjp(scaled_norm, kept["hidden_in"], gain_rows[0])[1](
            grad_normed
        )
        grad_hidden_b = (grad_hidden + grad_front).astype(BF)
        gain_vec = jnp.concatenate(
            [
                grad_gain0,
                grad_gain1,
                grad_gain2,
                grad_gain3,
                grad_gain4,
                grad_gain5,
                grad_query_gain,
                grad_key_gain,
            ]
        )
        late = jnp.concatenate([grad_q_b, grad_kv_b, grad_z_b], axis=1)
        return grad_hidden_b, late, ff_base, gain_vec

    near_0, near_1 = [], []
    background.add(near_units(0, last_block, near_0))
    out_0, kept_0 = forward(0, hidden_b, near_0)
    background.add(near_units(1, out_0, near_1))
    out_1, kept_1 = forward(1, out_0, near_1)
    normed_all_0 = lax.all_gather(
        tie(kept_0["normed_b"], rows_1_own)[0], "shard", axis=0, tiled=True
    )
    normed_all_1 = lax.all_gather(
        tie(kept_1["normed_b"], normed_all_0)[0], "shard", axis=0, tiled=True
    )
    top = pick(cotangent[0], cotangent[1])
    passed_0, passed_1, early_0, early_1, sides = [], [], [], [], []
    due_1 = [sides, normed_all_0, lambda work: work]
    grad_1, late_1, ff_base_1, gain_vec_1 = backward(1, kept_1, top, passed_1, early_1, due_1)
    normed_all_0 = due_1[1]

    def table_grads(work):
        side_all, normed_all = work
        return dot_first(one_hot, side_all), normed_all

    def gather_sides():
        keep = pick(sides[1], sides[0])
        other = swap_cores(pick(sides[0], sides[1]))
        two = jnp.concatenate([pick(keep, other), pick(other, keep)], axis=0)
        return lax.all_gather(two, "shard", axis=0, tiled=True)

    due_0 = [sides, None, table_grads]
    due_0_start = lambda: (gather_sides(), normed_all_1)
    due_0[1] = due_0_start
    grad_0, late_0, ff_base_0, gain_vec_0 = backward(0, kept_0, grad_1, passed_0, early_0, due_0)
    table_grad, normed_all_1 = due_0[1]

    def to_owners(late):
        padded = jnp.pad(late, ((0, 0), (0, n * rows_dev - IN_ROWS)))
        return padded.reshape(seq, n, rows_dev).transpose(1, 0, 2)

    gain_terms = jnp.concatenate(
        [gain_vec_0.reshape(n, gains_dev), gain_vec_1.reshape(n, gains_dev)], axis=1
    ).astype(BF)
    width = 2 * rows_dev
    gain_lines = -(-2 * gains_dev // width)
    gain_lines_padded = -(-gain_lines // 8) * 8
    gain_terms = jnp.pad(gain_terms, ((0, 0), (0, gain_lines_padded * width - 2 * gains_dev)))
    outgoing = jnp.concatenate(
        [
            jnp.concatenate([to_owners(late_0), to_owners(late_1)], axis=2),
            gain_terms.reshape(n, gain_lines_padded, width),
        ],
        axis=1,
    )
    (outgoing, ff_base_0, ff_base_1, early_0[0]) = background.stage(
        outgoing, ff_base_0, ff_base_1, early_0[0]
    )
    incoming = lax.all_to_all(outgoing, "shard", 0, 0, tiled=True)
    late_sums = [
        dot_first(
            incoming[:, :seq, layer * rows_dev : (layer + 1) * rows_dev].reshape(
                n * seq, rows_dev
            ),
            normed_all,
        )
        for layer, normed_all in enumerate((normed_all_0, normed_all_1))
    ]
    run(early_rows(early_0.pop(), early_0))
    background.drain()
    early_keep = pick(early_0[0], early_1[0])
    early_other = swap_cores(pick(early_1[0], early_0[0]))
    attn_grad = (
        pick(late_sums[0], late_sums[1])
        + swap_cores(pick(late_sums[1], late_sums[0]).astype(BF)).astype(F32)
        + rejoin(early_keep, early_other, core)
    )
    gain_sums = jnp.sum(incoming[:, seq:].astype(F32), axis=0).reshape(-1)
    gain_sums = (gain_sums[:gains_dev], gain_sums[gains_dev : 2 * gains_dev])
    gain_grad = pick(gain_sums[0], gain_sums[1]) + swap_cores(pick(gain_sums[1], gain_sums[0]))

    def whole_ff(base, passed):
        passed = jnp.stack(passed)
        zeros = jnp.zeros((3, units - half_units, D), BF)
        placed = pick(
            jnp.concatenate([passed, zeros], axis=1), jnp.concatenate([zeros, passed], axis=1)
        )
        return base.astype(F32) + placed.astype(F32)

    whole_0, whole_1 = whole_ff(ff_base_0, passed_0), whole_ff(ff_base_1, passed_1)
    ff_grad = pick(whole_0, whole_1) + swap_cores(pick(whole_1, whole_0).astype(BF)).astype(F32)

    def outputs_of(value_0, value_1):
        keep = pick(value_0, value_1)
        other = swap_cores(pick(value_1, value_0))
        return jnp.stack([pick(keep, other), pick(other, keep)])

    return (
        outputs_of(out_0, out_1)[None],
        outputs_of(grad_0, grad_1)[None],
        attn_grad[None],
        ff_grad[None],
        gain_grad[None],
        table_grad[None],
    )


def solution(mesh):
    placed = (
        P(None, "shard", None),
        P(None, "shard", None),
        P(),
        P(None, "shard"),
        P("section", "shard", None),
        P("section", None, "shard", None),
        P("section", "shard"),
        P("section", "shard", None),
    )
    return jax.shard_map(
        per_device,
        mesh=mesh,
        in_specs=placed,
        out_specs=(
            P("section", None, "shard", None),
            P("section", None, "shard", None),
            P("section", "shard", None),
            P("section", None, "shard", None),
            P("section", "shard"),
            P("section", "shard", None),
        ),
        check_vma=False,
    )
```

```python
import itertools
import math
from functools import partial

import jax
import jax.numpy as jnp
from jax import lax
from jax.sharding import PartitionSpec as P

D = 2048
HEADS = 8
KV_HEADS = 2
HEAD_DIM = 256
RANK = 64
PLD = 256
HALF = D // 2
QW = HEADS * HEAD_DIM
KW = KV_HEADS * HEAD_DIM
IN_ROWS = QW + 2 * KW + RANK
OUT_START = IN_ROWS + PLD
LAUREL_START = OUT_START + QW
SIDE_START = LAUREL_START + RANK

EPS = 1e-06
ROPE_BASE = 10000.0
INV_ROOT2 = 0.7071067811865476
MASKED = -1e30
SCALE = HEAD_DIM ** (-0.5)
BF = jnp.bfloat16
F32 = jnp.float32

ALL_CHIPS = ((0, 2, 1), (0, 1, 2))
PLANE = ((0, 1), (0, 1))


def tie(*values):
    return lax.optimization_barrier(values)


def chip_dims(n):
    side = math.isqrt(n // 4)
    return (4, side, side)


def chip_strides(n):
    sizes = chip_dims(n)
    return (sizes[1] * sizes[2], sizes[2], 1)


def hop(value, n, dims, step):
    sizes, strides = chip_dims(n), chip_strides(n)
    pairs = []
    for core, dim in enumerate(dims):
        for i in range(n):
            place = (i // strides[dim]) % sizes[dim]
            target = i + ((place + step) % sizes[dim] - place) * strides[dim]
            pairs.append((core * n + i, core * n + target))
    return lax.ppermute(value, ("section", "shard"), pairs)


def swap_cores(value):
    return lax.ppermute(value, "section", [(0, 1), (1, 0)])


def offsets_of(n, orders):
    sizes = chip_dims(n)
    return list(itertools.product(*[range(sizes[d]) for d in orders[0]]))


def tree(n, orders):
    rounds = {}
    for offset in offsets_of(n, orders):
        if sum(offset) > 0:
            last = max(i for i, steps in enumerate(offset) if steps > 0)
            parent = tuple(steps - (i == last) for i, steps in enumerate(offset))
            edge = (offset, parent, (orders[0][last], orders[1][last]))
            rounds.setdefault(sum(offset), []).append(edge)
    return [rounds[number] for number in sorted(rounds)]


def source_index(me, core, n, orders, offset):
    sizes, strides = chip_dims(n), chip_strides(n)
    found = []
    for order in orders:
        index = me
        for dim, steps in zip(order, offset):
            place = (me // strides[dim]) % sizes[dim]
            index = index + ((place - steps) % sizes[dim] - place) * strides[dim]
        found.append(index)
    return jnp.where(core == 0, found[0], found[1])


def gather_tree(block, n, orders):
    found = {(0,) * len(orders[0]): block}
    for edges in tree(n, orders):
        for offset, parent, dims in edges:
            found[offset] = hop(found[parent], n, dims, 1)
    return found


def scatter_steps(terms, n, orders, sums, beside=None):
    totals = dict(terms)
    for number, edges in enumerate(reversed(tree(n, orders))):
        sent = [hop(totals[offset].astype(BF), n, dims, -1) for offset, _, dims in edges]
        if number == 1 and beside is not None:
            sent = beside(sent)
        sent, _ = yield sent
        for (_, parent, _), value in zip(edges, sent):
            totals[parent] = totals[parent].astype(F32) + value.astype(F32)
    sums.append(totals[(0,) * len(orders[0])])


def run(job):
    sent = next(job)
    while True:
        try:
            sent = job.send((sent, None))
        except StopIteration:
            return


def scatter_tree(terms, n, orders):
    sums = []
    run(scatter_steps(terms, n, orders, sums))
    return sums[0]


class Background:
    def __init__(self):
        self.jobs = []

    def add(self, job):
        self.jobs.append((job, next(job)))

    def stage(self, *values):
        values, flying = lax.optimization_barrier((values, [sent for _, sent in self.jobs]))
        going = []
        for (job, _), sent in zip(self.jobs, flying):
            try:
                going.append((job, job.send((sent, values[0]))))
            except StopIteration:
                pass
        self.jobs = going
        return values

    def drain(self):
        while self.jobs:
            going = []
            for job, sent in self.jobs:
                try:
                    going.append((job, job.send((sent, None))))
                except StopIteration:
                    pass
            self.jobs = going


def after(value, anchor):
    return value if anchor is None else tie(value, anchor)[0]


def gather_small(value, me, n):
    step = 1
    while step < n:
        other = lax.ppermute(value, "shard", [(i, i ^ step) for i in range(n)])
        lower = (me // step) % 2 == 0
        value = jnp.where(
            lower,
            jnp.concatenate([value, other], axis=0),
            jnp.concatenate([other, value], axis=0),
        )
        step *= 2
    return value


def rms_norm(values):
    return values * lax.rsqrt(jnp.mean(values * values, axis=-1, keepdims=True) + EPS)


def scaled_norm(values, gain_vec):
    return rms_norm(values) * gain_vec


def rope_tables(positions):
    half_width = HEAD_DIM // 2
    frequency = ROPE_BASE ** (-jnp.arange(half_width, dtype=F32) * (2.0 / HEAD_DIM))
    angles = positions.astype(F32)[:, None] * frequency[None, :]
    return (jnp.cos(angles), jnp.sin(angles))


def rotate(vectors, cosine_part, sine_part):
    half_width = vectors.shape[-1] // 2
    first_half = vectors[..., :half_width]
    second_half = vectors[..., half_width:]
    cosine_rows = cosine_part[:, None, :]
    sine_rows = sine_part[:, None, :]
    return jnp.concatenate(
        [
            first_half * cosine_rows - second_half * sine_rows,
            second_half * cosine_rows + first_half * sine_rows,
        ],
        axis=-1,
    )


def query_heads(projected, query_gain, cosine_part, sine_part):
    heads = projected.reshape(projected.shape[0], HEADS, HEAD_DIM)
    return rotate(rms_norm(heads) * query_gain, cosine_part, sine_part)


def key_value_heads(projected, key_gain, cosine_part, sine_part):
    row_count = projected.shape[0]
    key_heads = projected[:, :KW].reshape(row_count, KV_HEADS, HEAD_DIM)
    value_heads = projected[:, KW:].reshape(row_count, KV_HEADS, HEAD_DIM)
    key_heads = rotate(rms_norm(key_heads) * key_gain, cosine_part, sine_part)
    return jnp.concatenate(
        [key_heads.reshape(row_count, KW), rms_norm(value_heads).reshape(row_count, KW)], axis=1
    )


def join_piece(hidden_in, normed, attended, laurel_raw, gain_laurel, gain_attn, gain_ffin):
    joined = (
        hidden_in + rms_norm(attended) * gain_attn + normed + rms_norm(laurel_raw) * gain_laurel
    ) * INV_ROOT2
    return (joined, rms_norm(joined) * gain_ffin)


def gated_gelu(gate_pre, up_pre):
    return jax.nn.gelu(gate_pre, approximate=True) * up_pre


def add_branch(residual, branch, gain_out):
    return residual + rms_norm(branch) * gain_out


def dot(left_side, right_side):
    return jnp.dot(left_side, right_side, preferred_element_type=F32)


def dot_rows(left_side, right_side):
    return lax.dot_general(
        left_side, right_side, (((1,), (1,)), ((), ())), preferred_element_type=F32
    )


def dot_first(left_side, right_side):
    return lax.dot_general(
        left_side, right_side, (((0,), (0,)), ((), ())), preferred_element_type=F32
    )


def halves(value, core):
    left, right = value[..., :HALF], value[..., HALF:]
    return jnp.where(core == 0, left, right), jnp.where(core == 0, right, left)


def rejoin(own, other, core):
    return jnp.concatenate(
        [jnp.where(core == 0, own, other), jnp.where(core == 0, other, own)], axis=-1
    )


def rows_product(value, rows, start, stop, core):
    own, other = halves(value, core)
    return dot_rows(own, rows[0][start:stop]) + dot_rows(other, rows[1][start:stop])


def back_product(value, rows, start, stop, core):
    return rejoin(dot(value, rows[0][start:stop]), dot(value, rows[1][start:stop]), core)


def per_device(tokens, cotangent, block_ids, token_ids, attn_weight, ff_weight, gains, table):
    core = lax.axis_index("section")
    me = lax.axis_index("shard")
    n = lax.axis_size("shard")
    seq = tokens.shape[1]
    rows_dev = attn_weight.shape[1]
    units = ff_weight.shape[2]
    half_units = units // 2
    gains_dev = gains.shape[1]
    vocab_dev = table.shape[1]
    side = chip_dims(n)[2]
    background = Background()

    def pick(for_0, for_1):
        return jnp.where(core == 0, for_0, for_1)

    def by_layer(mine, theirs):
        return (pick(mine, theirs), pick(theirs, mine))

    gain_pair = by_layer(gains[0].astype(F32), swap_cores(gains[0]).astype(F32))
    small = jnp.concatenate([gain_pair[0], gain_pair[1], token_ids.reshape(-1).astype(F32)])
    small_all = gather_small(small[None], me, n)
    layer_gains = [
        small_all[:, layer * gains_dev : (layer + 1) * gains_dev].reshape(n * gains_dev)
        for layer in range(2)
    ]
    all_ids = small_all[:, 2 * gains_dev :].astype(jnp.int32).reshape(-1)

    one_hot = (
        (all_ids - me * vocab_dev)[:, None] == jnp.arange(vocab_dev, dtype=jnp.int32)[None, :]
    ).astype(BF)
    looked_up = dot(one_hot, table[0]).astype(BF)

    own_half, other_half = halves(attn_weight[0], core)
    attn_blocks = by_layer(own_half, swap_cores(other_half))
    rows_1_own = lax.all_gather(attn_blocks[1], "shard", axis=0, tiled=True)
    ff_own = by_layer(ff_weight[0], swap_cores(ff_weight[0]))
    ff_half = [lax.dynamic_slice_in_dim(own, core * half_units, half_units, 1) for own in ff_own]
    buffers = [jnp.zeros((n, rows_dev, HALF), BF), jnp.zeros((n, rows_dev, HALF), BF)]

    def store_blocks(buffers, fresh):
        for offset, block in fresh.items():
            sources = [source_index(me, c, n, ALL_CHIPS, offset) for c in (core, 1 - core)]
            buffers = [
                lax.dynamic_update_slice(
                    buffer, value[None], (source, jnp.int32(0), jnp.int32(0))
                )
                for buffer, value, source in zip(buffers, (block, swap_cores(block)), sources)
            ]
        return buffers

    fresh = {(0, 0, 0): attn_blocks[0]}
    held = dict(fresh)
    for number, edges in enumerate(tree(n, ALL_CHIPS)):
        arriving = {offset: hop(held[parent], n, dims, 1) for offset, parent, dims in edges}
        buffers = store_blocks(buffers, fresh)
        if number == 1:
            arriving, looked_up = tie(arriving, looked_up)
        if number == 2:
            arriving, ff_own = tie(arriving, ff_own)
        if number == 3:
            arriving, ff_half = tie(arriving, ff_half)
        fresh, held, buffers = tie(arriving, held, buffers)
        held.update(fresh)
    buffers = store_blocks(buffers, fresh)
    rows_0 = [buffer.reshape(n * rows_dev, HALF) for buffer in buffers]
    rows_1 = [rows_1_own, swap_cores(rows_1_own)]
    attn_rows = (rows_0, rows_1)
    looked_up = lax.psum_scatter(looked_up, "shard", scatter_dimension=0, tiled=True)
    looked_up = looked_up.reshape(2, seq, PLD)
    side_theirs = swap_cores(pick(looked_up[1], looked_up[0]))
    side_inputs = [
        value.astype(F32) for value in by_layer(pick(looked_up[0], looked_up[1]), side_theirs)
    ]

    positions = me * seq + jnp.arange(seq, dtype=jnp.int32)
    cosine_part, sine_part = rope_tables(positions)
    query_split = partial(query_heads, cosine_part=cosine_part, sine_part=sine_part)
    key_value_split = partial(key_value_heads, cosine_part=cosine_part, sine_part=sine_part)
    key_offsets = offsets_of(n, ALL_CHIPS)
    plane_offsets = offsets_of(n, PLANE)
    sources = jnp.stack([source_index(me, core, n, ALL_CHIPS, offset) for offset in key_offsets])
    blocks = pick(block_ids[0], block_ids[1]).reshape(n, seq)
    key_blocks = jnp.take(blocks, sources, axis=0).reshape(-1)
    allowed = key_blocks[None, :] <= key_blocks[:seq, None]
    hidden_b = pick(tokens[0], tokens[1])

    def near_units(layer, anchor, near):
        for which in range(3):
            current = after(ff_half[layer][which], anchor)
            parts = []
            for _ in range(side - 1):
                (current,), anchor = yield [hop(current, n, (2, 2), 1)]
                parts.append(current)
            near.append(parts)

    def plane_gather(value):
        found = gather_tree(value, n, PLANE)
        return jnp.concatenate([found[offset] for offset in plane_offsets], axis=0)

    def plane_scatter(value):
        terms = {o: value[i * seq : (i + 1) * seq] for i, o in enumerate(plane_offsets)}
        return scatter_tree(terms, n, PLANE)

    def split_gains(layer):
        flat = layer_gains[layer]
        return flat[: 6 * D].reshape(6, D), flat[6 * D : 6 * D + HEAD_DIM], flat[6 * D + HEAD_DIM :]

    def forward(layer, hidden_b, near):
        rows = attn_rows[layer]
        gain_rows, query_gain, key_gain = split_gains(layer)
        hidden_in = hidden_b.astype(F32)
        normed = scaled_norm(hidden_in, gain_rows[0])
        normed_b = normed.astype(BF)
        projected_kv = rows_product(normed_b, rows, QW, QW + 2 * KW, core)
        local = key_value_split(projected_kv, key_gain).astype(BF)
        (local,) = background.stage(local)
        if layer == 0:
            background.add(near_units(0, local, near))
        found = gather_tree(local, n, ALL_CHIPS)
        projected_q = rows_product(normed_b, rows, 0, QW, core)
        queries_b = query_split(projected_q, query_gain).astype(BF)
        queries_b = queries_b.reshape(seq, KV_HEADS, HEADS // KV_HEADS, HEAD_DIM)
        latent_b = rows_product(normed_b, rows, QW + 2 * KW, IN_ROWS, core).astype(BF)
        laurel_raw = back_product(latent_b, rows, LAUREL_START, SIDE_START, core)
        key_value = jnp.concatenate([found[offset] for offset in key_offsets], axis=0)
        key_value, queries_b, laurel_raw = background.stage(key_value, queries_b, laurel_raw)
        keys_b = key_value[:, :KW].reshape(-1, KV_HEADS, HEAD_DIM)
        values_b = key_value[:, KW:].reshape(-1, KV_HEADS, HEAD_DIM)
        scores = (
            jnp.einsum("qkgd,jkd->kgqj", queries_b, keys_b, preferred_element_type=F32) * SCALE
        )
        scores = jnp.where(allowed, scores, MASKED)
        row_max = jnp.max(scores, axis=-1, keepdims=True)
        exponentials = jnp.exp(scores - row_max)
        probabilities = exponentials / jnp.sum(exponentials, axis=-1, keepdims=True)
        mixed_b = (
            jnp.einsum(
                "kgqj,jkd->qkgd", probabilities.astype(BF), values_b, preferred_element_type=F32
            )
            .reshape(seq, QW)
            .astype(BF)
        )
        attended = back_product(mixed_b, rows, OUT_START, LAUREL_START, core)
        joined, prenorm = join_piece(
            hidden_in, normed, attended, laurel_raw, gain_rows[1], gain_rows[2], gain_rows[3]
        )
        (prenorm_b,) = background.stage(prenorm.astype(BF))
        prenorm_all = plane_gather(prenorm_b)
        (prenorm_all,) = background.stage(prenorm_all)
        while len(near) < 3:
            (prenorm_all,) = background.stage(prenorm_all)
        weights = [
            [ff_own[layer][which]]
            + [part for through in near[which] for part in (through, swap_cores(through))]
            for which in range(3)
        ]
        gate = [dot_rows(prenorm_all, part) for part in weights[0]]
        up = [dot_rows(prenorm_all, part) for part in weights[1]]
        hidden_ff_b = [gated_gelu(g, u).astype(BF) for g, u in zip(gate, up)]
        down_out = plane_scatter(sum(dot(h, part) for h, part in zip(hidden_ff_b, weights[2])))
        (down_out,) = background.stage(down_out)
        if layer == 0:
            background.add(near_units(1, down_out, near_1))
        settled = add_branch(joined, down_out, gain_rows[4])
        settled_b = settled.astype(BF)
        side_gate = rows_product(settled_b, rows, IN_ROWS, OUT_START, core)
        gated_b = gated_gelu(side_gate, side_inputs[layer]).astype(BF)
        projected = back_product(gated_b, rows, SIDE_START, SIDE_START + PLD, core)
        layer_out_b = add_branch(settled, projected, gain_rows[5]).astype(BF)
        return layer_out_b, dict(
            hidden_in=hidden_in,
            normed=normed,
            normed_b=normed_b,
            projected_q=projected_q,
            projected_kv=projected_kv,
            weights=weights,
            queries_b=queries_b,
            keys_b=keys_b,
            values_b=values_b,
            probabilities=probabilities,
            mixed_b=mixed_b,
            attended=attended,
            latent_b=latent_b,
            laurel_raw=laurel_raw,
            joined=joined,
            prenorm_all=prenorm_all,
            gate=gate,
            up=up,
            hidden_ff_b=hidden_ff_b,
            down_out=down_out,
            settled=settled,
            settled_b=settled_b,
            side_gate=side_gate,
            gated_b=gated_b,
            projected=projected,
        )

    def early_products(pairs):
        lefts = jnp.concatenate([left for left, _ in pairs], axis=1)
        lefts = jnp.concatenate([lefts, swap_cores(lefts)], axis=0)
        own, other = halves(jnp.stack([right for _, right in pairs]), core)
        rights = jnp.concatenate([own, swap_cores(other)], axis=1)
        terms = [jnp.zeros((IN_ROWS - upper_rows, HALF), BF)]
        start = 0
        for i, (left, _) in enumerate(pairs):
            stop = start + left.shape[1]
            terms.append(dot_first(lefts[:, start:stop], rights[i]).astype(BF))
            start = stop
        return jnp.concatenate(terms, axis=0)

    first = (rows_dev // 2 + 7) // 8 * 8
    upper_rows = n // 2 * rows_dev

    def early_rows(term, result, beside=None, finish=None):
        shaped = term.reshape(n // 2, rows_dev, HALF)
        upper = me >= n // 2
        pieces = {}
        for offset in key_offsets:
            target = source_index(me, core, n, ALL_CHIPS, offset)
            place = (target % (n // 2), jnp.where(target >= n // 2, 0, rows_dev - first), 0)
            pieces[offset] = lax.dynamic_slice(shaped, place, (1, first, HALF))[0]
        sums = []
        yield from scatter_steps(pieces, n, ALL_CHIPS, sums, beside)
        mine = sums[0].astype(BF)
        if finish is not None:
            mine = finish(mine)
        sent = lax.ppermute(mine, "shard", [(i, i + n // 2) for i in range(n // 2)])
        (sent,), _ = yield [sent]
        whole = jnp.concatenate([mine, sent[2 * first - rows_dev :]], axis=0).astype(F32)
        result.append(jnp.where(upper, whole, 0.0))

    def backward(layer, kept, grad_out_b, passed, early, due):
        rows = attn_rows[layer]
        weights = kept["weights"]
        gain_rows, query_gain, key_gain = split_gains(layer)
        grad_out = grad_out_b.astype(F32)
        grad_settled, grad_projected, grad_gain5 = jax.vjp(
            add_branch, kept["settled"], kept["projected"], gain_rows[5]
        )[1](grad_out)
        grad_projected_b = grad_projected.astype(BF)
        grad_gated = rows_product(grad_projected_b, rows, SIDE_START, SIDE_START + PLD, core)
        grad_side_gate, grad_side = jax.vjp(gated_gelu, kept["side_gate"], side_inputs[layer])[1](
            grad_gated
        )
        grad_side_gate_b = grad_side_gate.astype(BF)
        grad_settled = grad_settled + back_product(
            grad_side_gate_b, rows, IN_ROWS, OUT_START, core
        )
        grad_joined, grad_down, grad_gain4 = jax.vjp(
            add_branch, kept["joined"], kept["down_out"], gain_rows[4]
        )[1](grad_settled)
        due[0].append(grad_side.astype(BF))
        (grad_down_b,) = background.stage(grad_down.astype(BF))
        grad_down_all = plane_gather(grad_down_b)
        (grad_down_all,) = background.stage(grad_down_all)
        grad_hidden_ff = [dot_rows(grad_down_all, part) for part in weights[2]]
        grad_gate_up = [
            jax.vjp(gated_gelu, g, u)[1](grad)
            for g, u, grad in zip(kept["gate"], kept["up"], grad_hidden_ff)
        ]
        grad_gate_b = [pair[0].astype(BF) for pair in grad_gate_up]
        grad_up_b = [pair[1].astype(BF) for pair in grad_gate_up]
        grad_prenorm = sum(
            dot(g, wg) + dot(u, wu)
            for g, u, wg, wu in zip(grad_gate_b, grad_up_b, weights[0], weights[1])
        )
        grad_prenorm, grad_gate_b, grad_up_b = tie(grad_prenorm, grad_gate_b, grad_up_b)
        grad_prenorm = plane_scatter(grad_prenorm)
        ff_terms = [
            [dot_first(g, kept["prenorm_all"]).astype(BF) for g in grad_gate_b],
            [dot_first(u, kept["prenorm_all"]).astype(BF) for u in grad_up_b],
            [dot_first(h, grad_down_all).astype(BF) for h in kept["hidden_ff_b"]],
        ]
        ff_base = jnp.stack([terms[0] for terms in ff_terms])
        pair_sums = [
            [
                (terms[1 + 2 * i].astype(F32) + swap_cores(terms[2 + 2 * i]).astype(F32)).astype(BF)
                for i in range(side - 1)
            ]
            for terms in ff_terms
        ]
        grad_prenorm, pair_sums, ff_base = background.stage(grad_prenorm, pair_sums, ff_base)

        def pass_back():
            anchor = None
            for which in range(3):
                carried = None
                for steps in range(side - 1, 0, -1):
                    term = after(pair_sums[which][steps - 1], anchor)
                    if carried is not None:
                        term = (term.astype(F32) + carried.astype(F32)).astype(BF)
                    (carried,), anchor = yield [hop(term, n, (2, 2), -1)]
                passed.append(carried)

        background.add(pass_back())
        join_pull = jax.vjp(
            join_piece,
            kept["hidden_in"],
            kept["normed"],
            kept["attended"],
            kept["laurel_raw"],
            gain_rows[1],
            gain_rows[2],
            gain_rows[3],
        )[1]
        grad_hidden, grad_normed, grad_attended, grad_laurel, grad_gain1, grad_gain2, grad_gain3 = (
            join_pull((grad_joined, grad_prenorm))
        )
        grad_attended_b = grad_attended.astype(BF)
        grad_laurel_b = grad_laurel.astype(BF)
        grad_mixed_b = rows_product(grad_attended_b, rows, OUT_START, LAUREL_START, core).astype(BF)
        grad_latent = rows_product(grad_laurel_b, rows, LAUREL_START, SIDE_START, core)
        grad_mixed_heads = grad_mixed_b.reshape(seq, KV_HEADS, HEADS // KV_HEADS, HEAD_DIM)
        probabilities = kept["probabilities"]
        grad_probs = jnp.einsum(
            "qkgd,jkd->kgqj", grad_mixed_heads, kept["values_b"], preferred_element_type=F32
        )
        row_dot = jnp.sum(grad_probs * probabilities, axis=-1, keepdims=True)
        grad_scores_b = (probabilities * (grad_probs - row_dot)).astype(BF)
        grad_keys_all = (
            jnp.einsum(
                "kgqj,qkgd->jkd", grad_scores_b, kept["queries_b"], preferred_element_type=F32
            )
            * SCALE
        )
        grad_values_all = jnp.einsum(
            "kgqj,qkgd->jkd",
            probabilities.astype(BF),
            grad_mixed_heads,
            preferred_element_type=F32,
        )
        grad_key_value = jnp.concatenate(
            [grad_keys_all.reshape(-1, KW), grad_values_all.reshape(-1, KW)], axis=1
        ).astype(BF)
        early_pairs = (
            (grad_side_gate_b, kept["settled_b"]),
            (kept["mixed_b"], grad_attended_b),
            (kept["latent_b"], grad_laurel_b),
            (kept["gated_b"], grad_projected_b),
        )
        work = due[1]() if callable(due[1]) else due[1]
        grad_key_value, early_pairs, work = background.stage(grad_key_value, early_pairs, work)
        early_term = early_products(early_pairs)
        due[1] = due[2](work)
        terms = {o: grad_key_value[i * seq : (i + 1) * seq] for i, o in enumerate(key_offsets)}
        grad_local = scatter_tree(terms, n, ALL_CHIPS)
        grad_queries = (
            jnp.einsum("kgqj,jkd->qkgd", grad_scores_b, kept["keys_b"], preferred_element_type=F32)
            * SCALE
        )
        grad_projected_q, grad_query_gain = jax.vjp(query_split, kept["projected_q"], query_gain)[
            1
        ](grad_queries.reshape(seq, HEADS, HEAD_DIM))
        grad_q_b, grad_z_b = grad_projected_q.astype(BF), grad_latent.astype(BF)
        grad_normed = (
            grad_normed
            + back_product(grad_q_b, rows, 0, QW, core)
            + back_product(grad_z_b, rows, QW + 2 * KW, IN_ROWS, core)
        )
        grad_local, grad_normed, early_term, due[1] = background.stage(
            grad_local, grad_normed, early_term, due[1]
        )
        if layer == 1:
            background.add(early_rows(early_term, early))
        else:
            early.append(early_term)
        grad_projected_kv, grad_key_gain = jax.vjp(
            key_value_split, kept["projected_kv"], key_gain
        )[1](grad_local)
        grad_kv_b = grad_projected_kv.astype(BF)
        grad_normed = grad_normed + back_product(grad_kv_b, rows, QW, QW + 2 * KW, core)
        grad_front, grad_gain0 = jax.vjp(scaled_norm, kept["hidden_in"], gain_rows[0])[1](
            grad_normed
        )
        grad_hidden_b = (grad_hidden + grad_front).astype(BF)
        gain_vec = jnp.concatenate(
            [
                grad_gain0,
                grad_gain1,
                grad_gain2,
                grad_gain3,
                grad_gain4,
                grad_gain5,
                grad_query_gain,
                grad_key_gain,
            ]
        )
        late = jnp.concatenate([grad_q_b, grad_kv_b, grad_z_b], axis=1)
        return grad_hidden_b, late, ff_base, gain_vec

    near_0, near_1 = [], []
    out_0, kept_0 = forward(0, hidden_b, near_0)
    out_1, kept_1 = forward(1, out_0, near_1)
    normed_all_0 = lax.all_gather(kept_0["normed_b"], "shard", axis=0, tiled=True)
    top = pick(cotangent[0], cotangent[1])
    passed_0, passed_1, early_0, early_1, sides = [], [], [], [], []
    due_1 = [sides, normed_all_0, lambda work: work]
    grad_1, late_1, ff_base_1, gain_vec_1 = backward(1, kept_1, top, passed_1, early_1, due_1)
    normed_all_0 = due_1[1]
    grad_1, normed_b = tie(grad_1, kept_1["normed_b"])
    normed_all_1 = lax.all_gather(normed_b, "shard", axis=0, tiled=True)

    def table_product(side_all):
        return dot_first(one_hot, side_all)

    def gather_sides():
        keep = pick(sides[1], sides[0])
        other = swap_cores(pick(sides[0], sides[1]))
        two = jnp.concatenate([pick(keep, other), pick(other, keep)], axis=0)
        return lax.all_gather(two, "shard", axis=0, tiled=True)

    due_0 = [sides, None, lambda work: (table_product(work[0]), work[1])]
    due_0_start = lambda: (gather_sides(), normed_all_1)
    due_0[1] = due_0_start
    grad_0, late_0, ff_base_0, gain_vec_0 = backward(0, kept_0, grad_1, passed_0, early_0, due_0)
    table_grad, normed_all_1 = due_0[1]

    def to_owners(late):
        padded = jnp.pad(late, ((0, 0), (0, n * rows_dev - IN_ROWS)))
        return padded.reshape(seq, n, rows_dev).transpose(1, 0, 2)

    gain_terms = jnp.concatenate(
        [gain_vec_0.reshape(n, gains_dev), gain_vec_1.reshape(n, gains_dev)], axis=1
    ).astype(BF)
    width = 2 * rows_dev
    gain_lines = -(-2 * gains_dev // width)
    gain_lines_padded = -(-gain_lines // 8) * 8
    gain_terms = jnp.pad(gain_terms, ((0, 0), (0, gain_lines_padded * width - 2 * gains_dev)))
    outgoing = jnp.concatenate(
        [
            jnp.concatenate([to_owners(late_0), to_owners(late_1)], axis=2),
            gain_terms.reshape(n, gain_lines_padded, width),
        ],
        axis=1,
    )
    incoming = lax.all_to_all(outgoing, "shard", 0, 0, tiled=True)
    background.drain()

    def whole_ff(base, passed):
        passed = jnp.concatenate([part[None] for part in passed], axis=0)
        zeros = jnp.zeros((3, units - half_units, D), BF)
        placed = pick(
            jnp.concatenate([passed, zeros], axis=1), jnp.concatenate([zeros, passed], axis=1)
        )
        return base.astype(F32) + placed.astype(F32)

    def finish_ff(base_0, passed_0, base_1, passed_1):
        whole_0, whole_1 = whole_ff(base_0, passed_0), whole_ff(base_1, passed_1)
        other = swap_cores(pick(whole_1, whole_0).astype(BF)).astype(F32)
        return pick(whole_0, whole_1) + other

    def late_rows(arrived):
        sums = [
            dot_first(
                arrived[:, :seq, layer * rows_dev : (layer + 1) * rows_dev].reshape(
                    n * seq, rows_dev
                ),
                normed_all,
            )
            for layer, normed_all in enumerate((normed_all_0, normed_all_1))
        ]
        return pick(sums[0], sums[1]) + swap_cores(pick(sums[1], sums[0]).astype(BF)).astype(F32)

    ready = []

    def beside(sent):
        sent, parts = tie(sent, (ff_base_0, passed_0, ff_base_1, passed_1))
        ready.append(finish_ff(*parts))
        return sent

    def finish(mine):
        ready.append(late_rows(incoming))
        mine, ready[:] = tie(mine, list(ready))
        return mine

    run(early_rows(early_0.pop(), early_0, beside, finish))
    ff_grad, late_grad = ready
    early_keep = pick(early_0[0], early_1[0])
    early_other = swap_cores(pick(early_1[0], early_0[0]))
    attn_grad = (
        late_grad
        + rejoin(early_keep, early_other, core)
    )
    gain_sums = jnp.sum(incoming[:, seq:].astype(F32), axis=0).reshape(-1)
    gain_sums = (gain_sums[:gains_dev], gain_sums[gains_dev : 2 * gains_dev])
    gain_grad = pick(gain_sums[0], gain_sums[1]) + swap_cores(pick(gain_sums[1], gain_sums[0]))

    def outputs_of(value_0, value_1):
        keep = pick(value_0, value_1)
        other = swap_cores(pick(value_1, value_0))
        return jnp.stack([pick(keep, other), pick(other, keep)])

    return (
        outputs_of(out_0, out_1)[None],
        outputs_of(grad_0, grad_1)[None],
        attn_grad[None],
        ff_grad[None],
        gain_grad[None],
        table_grad[None],
    )


def solution(mesh):
    placed = (
        P(None, "shard", None),
        P(None, "shard", None),
        P(),
        P(None, "shard"),
        P("section", "shard", None),
        P("section", None, "shard", None),
        P("section", "shard"),
        P("section", "shard", None),
    )
    return jax.shard_map(
        per_device,
        mesh=mesh,
        in_specs=placed,
        out_specs=(
            P("section", None, "shard", None),
            P("section", None, "shard", None),
            P("section", "shard", None),
            P("section", None, "shard", None),
            P("section", "shard"),
            P("section", "shard", None),
        ),
        check_vma=False,
    )
```

```python
import itertools
import math
from functools import partial

import jax
import jax.numpy as jnp
from jax import lax
from jax.sharding import PartitionSpec as P

D = 2048
HEADS = 8
KV_HEADS = 2
HEAD_DIM = 256
RANK = 64
PLD = 256
HALF = D // 2
QW = HEADS * HEAD_DIM
KW = KV_HEADS * HEAD_DIM
IN_ROWS = QW + 2 * KW + RANK
OUT_START = IN_ROWS + PLD
LAUREL_START = OUT_START + QW
SIDE_START = LAUREL_START + RANK

EPS = 1e-06
ROPE_BASE = 10000.0
INV_ROOT2 = 0.7071067811865476
MASKED = -1e30
SCALE = HEAD_DIM ** (-0.5)
BF = jnp.bfloat16
F32 = jnp.float32

ALL_CHIPS = ((0, 2, 1), (0, 1, 2))
PLANE = ((0, 1), (0, 1))


def tie(*values):
    return lax.optimization_barrier(values)


def chip_dims(n):
    side = math.isqrt(n // 4)
    return (4, side, side)


def chip_strides(n):
    sizes = chip_dims(n)
    return (sizes[1] * sizes[2], sizes[2], 1)


def hop(value, n, dims, step):
    sizes, strides = chip_dims(n), chip_strides(n)
    pairs = []
    for core, dim in enumerate(dims):
        for i in range(n):
            place = (i // strides[dim]) % sizes[dim]
            target = i + ((place + step) % sizes[dim] - place) * strides[dim]
            pairs.append((core * n + i, core * n + target))
    return lax.ppermute(value, ("section", "shard"), pairs)


def swap_cores(value):
    return lax.ppermute(value, "section", [(0, 1), (1, 0)])


def offsets_of(n, orders):
    sizes = chip_dims(n)
    return list(itertools.product(*[range(sizes[d]) for d in orders[0]]))


def tree(n, orders):
    rounds = {}
    for offset in offsets_of(n, orders):
        if sum(offset) > 0:
            last = max(i for i, steps in enumerate(offset) if steps > 0)
            parent = tuple(steps - (i == last) for i, steps in enumerate(offset))
            edge = (offset, parent, (orders[0][last], orders[1][last]))
            rounds.setdefault(sum(offset), []).append(edge)
    return [rounds[number] for number in sorted(rounds)]


def source_index(me, core, n, orders, offset):
    sizes, strides = chip_dims(n), chip_strides(n)
    found = []
    for order in orders:
        index = me
        for dim, steps in zip(order, offset):
            place = (me // strides[dim]) % sizes[dim]
            index = index + ((place - steps) % sizes[dim] - place) * strides[dim]
        found.append(index)
    return jnp.where(core == 0, found[0], found[1])


def gather_tree(block, n, orders):
    found = {(0,) * len(orders[0]): block}
    for edges in tree(n, orders):
        for offset, parent, dims in edges:
            found[offset] = hop(found[parent], n, dims, 1)
    return found


def scatter_steps(terms, n, orders, sums, finish=None, pieces=(), landed=None):
    totals = dict(terms)
    levels = tree(n, orders)
    for number, edges in enumerate(reversed(levels)):
        sent = [totals[offset].astype(BF) for offset, _, _ in edges]
        if finish is not None and edges is levels[0]:
            sent = finish(sent)
        if number < len(pieces):
            sent, piece = tie(sent, pieces[number])
            landed.append(hop(piece, n, (2, 2), -1))
        sent = [hop(value, n, dims, -1) for value, (_, _, dims) in zip(sent, edges)]
        sent, _ = yield sent
        for (_, parent, _), value in zip(edges, sent):
            totals[parent] = totals[parent].astype(F32) + value.astype(F32)
    sums.append(totals[(0,) * len(orders[0])])


def run(job):
    sent = next(job)
    while True:
        try:
            sent = job.send((sent, None))
        except StopIteration:
            return


def scatter_tree(terms, n, orders):
    sums = []
    run(scatter_steps(terms, n, orders, sums))
    return sums[0]


class Background:
    def __init__(self):
        self.jobs = []

    def add(self, job):
        self.jobs.append((job, next(job)))

    def stage(self, *values):
        values, flying = lax.optimization_barrier((values, [sent for _, sent in self.jobs]))
        going = []
        for (job, _), sent in zip(self.jobs, flying):
            try:
                going.append((job, job.send((sent, values[0]))))
            except StopIteration:
                pass
        self.jobs = going
        return values

    def drain(self):
        while self.jobs:
            going = []
            for job, sent in self.jobs:
                try:
                    going.append((job, job.send((sent, None))))
                except StopIteration:
                    pass
            self.jobs = going


def after(value, anchor):
    return value if anchor is None else tie(value, anchor)[0]


def gather_small(value, me, n):
    step = 1
    while step < n:
        other = lax.ppermute(value, "shard", [(i, i ^ step) for i in range(n)])
        lower = (me // step) % 2 == 0
        value = jnp.where(
            lower,
            jnp.concatenate([value, other], axis=0),
            jnp.concatenate([other, value], axis=0),
        )
        step *= 2
    return value


def rms_norm(values):
    return values * lax.rsqrt(jnp.mean(values * values, axis=-1, keepdims=True) + EPS)


def scaled_norm(values, gain_vec):
    return rms_norm(values) * gain_vec


def rope_tables(positions):
    half_width = HEAD_DIM // 2
    frequency = ROPE_BASE ** (-jnp.arange(half_width, dtype=F32) * (2.0 / HEAD_DIM))
    angles = positions.astype(F32)[:, None] * frequency[None, :]
    return (jnp.cos(angles), jnp.sin(angles))


def rotate(vectors, cosine_part, sine_part):
    half_width = vectors.shape[-1] // 2
    first_half = vectors[..., :half_width]
    second_half = vectors[..., half_width:]
    cosine_rows = cosine_part[:, None, :]
    sine_rows = sine_part[:, None, :]
    return jnp.concatenate(
        [
            first_half * cosine_rows - second_half * sine_rows,
            second_half * cosine_rows + first_half * sine_rows,
        ],
        axis=-1,
    )


def query_heads(projected, query_gain, cosine_part, sine_part):
    heads = projected.reshape(projected.shape[0], HEADS, HEAD_DIM)
    return rotate(rms_norm(heads) * query_gain, cosine_part, sine_part)


def key_value_heads(projected, key_gain, cosine_part, sine_part):
    row_count = projected.shape[0]
    key_heads = projected[:, :KW].reshape(row_count, KV_HEADS, HEAD_DIM)
    value_heads = projected[:, KW:].reshape(row_count, KV_HEADS, HEAD_DIM)
    key_heads = rotate(rms_norm(key_heads) * key_gain, cosine_part, sine_part)
    return jnp.concatenate(
        [key_heads.reshape(row_count, KW), rms_norm(value_heads).reshape(row_count, KW)], axis=1
    )


def join_piece(hidden_in, normed, attended, laurel_raw, gain_laurel, gain_attn, gain_ffin):
    joined = (
        hidden_in + rms_norm(attended) * gain_attn + normed + rms_norm(laurel_raw) * gain_laurel
    ) * INV_ROOT2
    return (joined, rms_norm(joined) * gain_ffin)


def gated_gelu(gate_pre, up_pre):
    return jax.nn.gelu(gate_pre, approximate=True) * up_pre


def add_branch(residual, branch, gain_out):
    return residual + rms_norm(branch) * gain_out


def dot(left_side, right_side):
    return jnp.dot(left_side, right_side, preferred_element_type=F32)


def dot_rows(left_side, right_side):
    return lax.dot_general(
        left_side, right_side, (((1,), (1,)), ((), ())), preferred_element_type=F32
    )


def dot_first(left_side, right_side):
    return lax.dot_general(
        left_side, right_side, (((0,), (0,)), ((), ())), preferred_element_type=F32
    )


def halves(value, core):
    left, right = value[..., :HALF], value[..., HALF:]
    return jnp.where(core == 0, left, right), jnp.where(core == 0, right, left)


def rejoin(own, other, core):
    return jnp.concatenate(
        [jnp.where(core == 0, own, other), jnp.where(core == 0, other, own)], axis=-1
    )


def rows_product(value, rows, start, stop, core):
    own, other = halves(value, core)
    return dot_rows(own, rows[0][start:stop]) + dot_rows(other, rows[1][start:stop])


def back_product(value, rows, start, stop, core):
    return rejoin(dot(value, rows[0][start:stop]), dot(value, rows[1][start:stop]), core)


def per_device(tokens, cotangent, block_ids, token_ids, attn_weight, ff_weight, gains, table):
    core = lax.axis_index("section")
    me = lax.axis_index("shard")
    n = lax.axis_size("shard")
    seq = tokens.shape[1]
    rows_dev = attn_weight.shape[1]
    units = ff_weight.shape[2]
    half_units = units // 2
    gains_dev = gains.shape[1]
    vocab_dev = table.shape[1]
    side = chip_dims(n)[2]
    background = Background()

    def pick(for_0, for_1):
        return jnp.where(core == 0, for_0, for_1)

    def by_layer(mine, theirs):
        return (pick(mine, theirs), pick(theirs, mine))

    gain_pair = by_layer(gains[0].astype(F32), swap_cores(gains[0]).astype(F32))
    small = jnp.concatenate([gain_pair[0], gain_pair[1], token_ids.reshape(-1).astype(F32)])
    small_all = gather_small(small[None], me, n)
    layer_gains = [
        small_all[:, layer * gains_dev : (layer + 1) * gains_dev].reshape(n * gains_dev)
        for layer in range(2)
    ]
    all_ids = small_all[:, 2 * gains_dev :].astype(jnp.int32).reshape(-1)

    one_hot = (
        (all_ids - me * vocab_dev)[:, None] == jnp.arange(vocab_dev, dtype=jnp.int32)[None, :]
    ).astype(BF)
    looked_up = dot(one_hot, table[0]).astype(BF)

    own_half, other_half = halves(attn_weight[0], core)
    attn_blocks = by_layer(own_half, swap_cores(other_half))
    rows_1_own = lax.all_gather(attn_blocks[1], "shard", axis=0, tiled=True)
    ff_own = by_layer(ff_weight[0], swap_cores(ff_weight[0]))
    ff_half = [lax.dynamic_slice_in_dim(own, core * half_units, half_units, 1) for own in ff_own]
    buffers = [jnp.zeros((n, rows_dev, HALF), BF), jnp.zeros((n, rows_dev, HALF), BF)]

    def store_blocks(buffers, fresh):
        for offset, block in fresh.items():
            sources = [source_index(me, c, n, ALL_CHIPS, offset) for c in (core, 1 - core)]
            buffers = [
                lax.dynamic_update_slice(
                    buffer, value[None], (source, jnp.int32(0), jnp.int32(0))
                )
                for buffer, value, source in zip(buffers, (block, swap_cores(block)), sources)
            ]
        return buffers

    fresh = {(0, 0, 0): attn_blocks[0]}
    held = dict(fresh)
    for number, edges in enumerate(tree(n, ALL_CHIPS)):
        arriving = {offset: hop(held[parent], n, dims, 1) for offset, parent, dims in edges}
        buffers = store_blocks(buffers, fresh)
        if number == 1:
            arriving, looked_up = tie(arriving, looked_up)
        if number == 2:
            arriving, ff_own = tie(arriving, ff_own)
        if number == 3:
            arriving, ff_half = tie(arriving, ff_half)
        fresh, held, buffers = tie(arriving, held, buffers)
        held.update(fresh)
    buffers = store_blocks(buffers, fresh)
    rows_0 = [buffer.reshape(n * rows_dev, HALF) for buffer in buffers]
    rows_1 = [rows_1_own, swap_cores(rows_1_own)]
    attn_rows = (rows_0, rows_1)
    looked_up = lax.psum_scatter(looked_up, "shard", scatter_dimension=0, tiled=True)
    looked_up = looked_up.reshape(2, seq, PLD)
    side_theirs = swap_cores(pick(looked_up[1], looked_up[0]))
    side_inputs = [
        value.astype(F32) for value in by_layer(pick(looked_up[0], looked_up[1]), side_theirs)
    ]

    positions = me * seq + jnp.arange(seq, dtype=jnp.int32)
    cosine_part, sine_part = rope_tables(positions)
    query_split = partial(query_heads, cosine_part=cosine_part, sine_part=sine_part)
    key_value_split = partial(key_value_heads, cosine_part=cosine_part, sine_part=sine_part)
    key_offsets = offsets_of(n, ALL_CHIPS)
    plane_offsets = offsets_of(n, PLANE)
    sources = jnp.stack([source_index(me, core, n, ALL_CHIPS, offset) for offset in key_offsets])
    blocks = pick(block_ids[0], block_ids[1]).reshape(n, seq)
    key_blocks = jnp.take(blocks, sources, axis=0).reshape(-1)
    allowed = key_blocks[None, :] <= key_blocks[:seq, None]
    hidden_b = pick(tokens[0], tokens[1])

    def near_units(layer, anchor, near):
        for which in range(3):
            current = after(ff_half[layer][which], anchor)
            parts = []
            for _ in range(side - 1):
                (current,), anchor = yield [hop(current, n, (2, 2), 1)]
                parts.append(current)
            near.append(parts)

    def plane_gather(value):
        found = gather_tree(value, n, PLANE)
        return jnp.concatenate([found[offset] for offset in plane_offsets], axis=0)

    def plane_scatter(value):
        terms = {o: value[i * seq : (i + 1) * seq] for i, o in enumerate(plane_offsets)}
        return scatter_tree(terms, n, PLANE)

    def split_gains(layer):
        flat = layer_gains[layer]
        return flat[: 6 * D].reshape(6, D), flat[6 * D : 6 * D + HEAD_DIM], flat[6 * D + HEAD_DIM :]

    def forward(layer, hidden_b, near):
        rows = attn_rows[layer]
        gain_rows, query_gain, key_gain = split_gains(layer)
        hidden_in = hidden_b.astype(F32)
        normed = scaled_norm(hidden_in, gain_rows[0])
        normed_b = normed.astype(BF)
        projected_kv = rows_product(normed_b, rows, QW, QW + 2 * KW, core)
        local = key_value_split(projected_kv, key_gain).astype(BF)
        (local,) = background.stage(local)
        if layer == 0:
            background.add(near_units(0, local, near))
        found = gather_tree(local, n, ALL_CHIPS)
        projected_q = rows_product(normed_b, rows, 0, QW, core)
        queries_b = query_split(projected_q, query_gain).astype(BF)
        queries_b = queries_b.reshape(seq, KV_HEADS, HEADS // KV_HEADS, HEAD_DIM)
        latent_b = rows_product(normed_b, rows, QW + 2 * KW, IN_ROWS, core).astype(BF)
        laurel_raw = back_product(latent_b, rows, LAUREL_START, SIDE_START, core)
        key_value = jnp.concatenate([found[offset] for offset in key_offsets], axis=0)
        key_value, queries_b, laurel_raw = background.stage(key_value, queries_b, laurel_raw)
        keys_b = key_value[:, :KW].reshape(-1, KV_HEADS, HEAD_DIM)
        values_b = key_value[:, KW:].reshape(-1, KV_HEADS, HEAD_DIM)
        scores = (
            jnp.einsum("qkgd,jkd->kgqj", queries_b, keys_b, preferred_element_type=F32) * SCALE
        )
        scores = jnp.where(allowed, scores, MASKED)
        row_max = jnp.max(scores, axis=-1, keepdims=True)
        exponentials = jnp.exp(scores - row_max)
        probabilities = exponentials / jnp.sum(exponentials, axis=-1, keepdims=True)
        mixed_b = (
            jnp.einsum(
                "kgqj,jkd->qkgd", probabilities.astype(BF), values_b, preferred_element_type=F32
            )
            .reshape(seq, QW)
            .astype(BF)
        )
        attended = back_product(mixed_b, rows, OUT_START, LAUREL_START, core)
        joined, prenorm = join_piece(
            hidden_in, normed, attended, laurel_raw, gain_rows[1], gain_rows[2], gain_rows[3]
        )
        (prenorm_b,) = background.stage(prenorm.astype(BF))
        prenorm_all = plane_gather(prenorm_b)
        (prenorm_all,) = background.stage(prenorm_all)
        while len(near) < 3:
            (prenorm_all,) = background.stage(prenorm_all)
        weights = [
            [ff_own[layer][which]]
            + [part for through in near[which] for part in (through, swap_cores(through))]
            for which in range(3)
        ]
        gate = [dot_rows(prenorm_all, part) for part in weights[0]]
        up = [dot_rows(prenorm_all, part) for part in weights[1]]
        hidden_ff_b = [gated_gelu(g, u).astype(BF) for g, u in zip(gate, up)]
        down_out = plane_scatter(sum(dot(h, part) for h, part in zip(hidden_ff_b, weights[2])))
        (down_out,) = background.stage(down_out)
        if layer == 0:
            background.add(near_units(1, down_out, near_1))
        settled = add_branch(joined, down_out, gain_rows[4])
        settled_b = settled.astype(BF)
        side_gate = rows_product(settled_b, rows, IN_ROWS, OUT_START, core)
        gated_b = gated_gelu(side_gate, side_inputs[layer]).astype(BF)
        projected = back_product(gated_b, rows, SIDE_START, SIDE_START + PLD, core)
        layer_out_b = add_branch(settled, projected, gain_rows[5]).astype(BF)
        return layer_out_b, dict(
            hidden_in=hidden_in,
            normed=normed,
            normed_b=normed_b,
            projected_q=projected_q,
            projected_kv=projected_kv,
            weights=weights,
            queries_b=queries_b,
            keys_b=keys_b,
            values_b=values_b,
            probabilities=probabilities,
            mixed_b=mixed_b,
            attended=attended,
            latent_b=latent_b,
            laurel_raw=laurel_raw,
            joined=joined,
            prenorm_all=prenorm_all,
            gate=gate,
            up=up,
            hidden_ff_b=hidden_ff_b,
            down_out=down_out,
            settled=settled,
            settled_b=settled_b,
            side_gate=side_gate,
            gated_b=gated_b,
            projected=projected,
        )

    def early_products(pairs):
        lefts = jnp.concatenate([left for left, _ in pairs], axis=1)
        lefts = jnp.concatenate([lefts, swap_cores(lefts)], axis=0)
        own, other = halves(jnp.stack([right for _, right in pairs]), core)
        rights = jnp.concatenate([own, swap_cores(other)], axis=1)
        terms = [jnp.zeros((IN_ROWS - upper_rows, HALF), BF)]
        start = 0
        for i, (left, _) in enumerate(pairs):
            stop = start + left.shape[1]
            terms.append(dot_first(lefts[:, start:stop], rights[i]).astype(BF))
            start = stop
        return jnp.concatenate(terms, axis=0)

    first = (rows_dev // 2 + 7) // 8 * 8
    upper_rows = n // 2 * rows_dev

    def early_rows(term, result, finish=None, riding=(), landed=None):
        shaped = term.reshape(n // 2, rows_dev, HALF)
        upper = me >= n // 2
        pieces = {}
        for offset in key_offsets:
            target = source_index(me, core, n, ALL_CHIPS, offset)
            place = (target % (n // 2), jnp.where(target >= n // 2, 0, rows_dev - first), 0)
            pieces[offset] = lax.dynamic_slice(shaped, place, (1, first, HALF))[0]
        sums = []
        yield from scatter_steps(pieces, n, ALL_CHIPS, sums, finish, riding, landed)
        mine = sums[0].astype(BF)
        sent = lax.ppermute(mine, "shard", [(i, i + n // 2) for i in range(n // 2)])
        (sent,), _ = yield [sent]
        whole = jnp.concatenate([mine, sent[2 * first - rows_dev :]], axis=0).astype(F32)
        result.append(jnp.where(upper, whole, 0.0))

    last_base, last_pieces = [], []

    def backward(layer, kept, grad_out_b, passed, early, due):
        rows = attn_rows[layer]
        weights = kept["weights"]
        gain_rows, query_gain, key_gain = split_gains(layer)
        grad_out = grad_out_b.astype(F32)
        grad_settled, grad_projected, grad_gain5 = jax.vjp(
            add_branch, kept["settled"], kept["projected"], gain_rows[5]
        )[1](grad_out)
        grad_projected_b = grad_projected.astype(BF)
        grad_gated = rows_product(grad_projected_b, rows, SIDE_START, SIDE_START + PLD, core)
        grad_side_gate, grad_side = jax.vjp(gated_gelu, kept["side_gate"], side_inputs[layer])[1](
            grad_gated
        )
        grad_side_gate_b = grad_side_gate.astype(BF)
        grad_settled = grad_settled + back_product(
            grad_side_gate_b, rows, IN_ROWS, OUT_START, core
        )
        grad_joined, grad_down, grad_gain4 = jax.vjp(
            add_branch, kept["joined"], kept["down_out"], gain_rows[4]
        )[1](grad_settled)
        due[0].append(grad_side.astype(BF))
        (grad_down_b,) = background.stage(grad_down.astype(BF))
        grad_down_all = plane_gather(grad_down_b)
        (grad_down_all,) = background.stage(grad_down_all)
        grad_hidden_ff = [dot_rows(grad_down_all, part) for part in weights[2]]
        grad_gate_up = [
            jax.vjp(gated_gelu, g, u)[1](grad)
            for g, u, grad in zip(kept["gate"], kept["up"], grad_hidden_ff)
        ]
        grad_gate_b = [pair[0].astype(BF) for pair in grad_gate_up]
        grad_up_b = [pair[1].astype(BF) for pair in grad_gate_up]
        grad_prenorm = sum(
            dot(g, wg) + dot(u, wu)
            for g, u, wg, wu in zip(grad_gate_b, grad_up_b, weights[0], weights[1])
        )
        grad_prenorm, grad_gate_b, grad_up_b = tie(grad_prenorm, grad_gate_b, grad_up_b)
        grad_prenorm = plane_scatter(grad_prenorm)
        ff_terms = [
            [dot_first(g, kept["prenorm_all"]).astype(BF) for g in grad_gate_b],
            [dot_first(u, kept["prenorm_all"]).astype(BF) for u in grad_up_b],
            [dot_first(h, grad_down_all).astype(BF) for h in kept["hidden_ff_b"]],
        ]
        ff_base = jnp.stack([terms[0] for terms in ff_terms])
        pair_sums = [
            [
                (terms[1 + 2 * i].astype(F32) + swap_cores(terms[2 + 2 * i]).astype(F32)).astype(BF)
                for i in range(side - 1)
            ]
            for terms in ff_terms
        ]
        grad_prenorm, pair_sums, ff_base = background.stage(grad_prenorm, pair_sums, ff_base)

        def pass_back(groups):
            anchor = None
            for group in groups:
                carried = None
                for steps in range(side - 1, 0, -1):
                    terms = [after(pair_sums[which][steps - 1], anchor) for which in group]
                    if carried is not None:
                        terms = [
                            (term.astype(F32) + part.astype(F32)).astype(BF)
                            for term, part in zip(terms, carried)
                        ]
                    carried, anchor = yield [hop(term, n, (2, 2), -1) for term in terms]
                passed.extend(carried)

        background.add(pass_back(((0, 1),) if layer == 0 else ((0,), (1,), (2,))))
        join_pull = jax.vjp(
            join_piece,
            kept["hidden_in"],
            kept["normed"],
            kept["attended"],
            kept["laurel_raw"],
            gain_rows[1],
            gain_rows[2],
            gain_rows[3],
        )[1]
        grad_hidden, grad_normed, grad_attended, grad_laurel, grad_gain1, grad_gain2, grad_gain3 = (
            join_pull((grad_joined, grad_prenorm))
        )
        grad_attended_b = grad_attended.astype(BF)
        grad_laurel_b = grad_laurel.astype(BF)
        grad_mixed_b = rows_product(grad_attended_b, rows, OUT_START, LAUREL_START, core).astype(BF)
        grad_latent = rows_product(grad_laurel_b, rows, LAUREL_START, SIDE_START, core)
        grad_mixed_heads = grad_mixed_b.reshape(seq, KV_HEADS, HEADS // KV_HEADS, HEAD_DIM)
        probabilities = kept["probabilities"]
        grad_probs = jnp.einsum(
            "qkgd,jkd->kgqj", grad_mixed_heads, kept["values_b"], preferred_element_type=F32
        )
        row_dot = jnp.sum(grad_probs * probabilities, axis=-1, keepdims=True)
        grad_scores_b = (probabilities * (grad_probs - row_dot)).astype(BF)
        grad_keys_all = (
            jnp.einsum(
                "kgqj,qkgd->jkd", grad_scores_b, kept["queries_b"], preferred_element_type=F32
            )
            * SCALE
        )
        grad_values_all = jnp.einsum(
            "kgqj,qkgd->jkd",
            probabilities.astype(BF),
            grad_mixed_heads,
            preferred_element_type=F32,
        )
        grad_key_value = jnp.concatenate(
            [grad_keys_all.reshape(-1, KW), grad_values_all.reshape(-1, KW)], axis=1
        ).astype(BF)
        early_pairs = (
            (grad_side_gate_b, kept["settled_b"]),
            (kept["mixed_b"], grad_attended_b),
            (kept["latent_b"], grad_laurel_b),
            (kept["gated_b"], grad_projected_b),
        )
        work = due[1]() if callable(due[1]) else due[1]
        grad_key_value, early_pairs, work, ff_base = background.stage(
            grad_key_value, early_pairs, work, ff_base
        )
        if layer == 0:
            ff_other = swap_cores(pick(last_base[0], ff_base))
        early_term = early_products(early_pairs)
        due[1] = due[2](work)
        terms = {o: grad_key_value[i * seq : (i + 1) * seq] for i, o in enumerate(key_offsets)}
        grad_local = scatter_tree(terms, n, ALL_CHIPS)
        grad_queries = (
            jnp.einsum("kgqj,jkd->qkgd", grad_scores_b, kept["keys_b"], preferred_element_type=F32)
            * SCALE
        )
        grad_projected_q, grad_query_gain = jax.vjp(query_split, kept["projected_q"], query_gain)[
            1
        ](grad_queries.reshape(seq, HEADS, HEAD_DIM))
        grad_q_b, grad_z_b = grad_projected_q.astype(BF), grad_latent.astype(BF)
        grad_normed = (
            grad_normed
            + back_product(grad_q_b, rows, 0, QW, core)
            + back_product(grad_z_b, rows, QW + 2 * KW, IN_ROWS, core)
        )
        if layer == 0:
            grad_local, grad_normed, early_term, due[1], pair_sums[2] = tie(
                grad_local, grad_normed, early_term, due[1], pair_sums[2]
            )
            if side == 2:
                last_pieces.extend(jnp.split(pair_sums[2][0], 4, axis=0))
            else:
                background.add(pass_back(((2,),)))
            ff_base = pick(ff_base, last_base[0]).astype(F32) + ff_other.astype(F32)
            early.append(early_term)
        else:
            grad_local, grad_normed, early_term, due[1] = background.stage(
                grad_local, grad_normed, early_term, due[1]
            )
            background.add(early_rows(early_term, early))
            last_base.append(ff_base)
        grad_projected_kv, grad_key_gain = jax.vjp(
            key_value_split, kept["projected_kv"], key_gain
        )[1](grad_local)
        grad_kv_b = grad_projected_kv.astype(BF)
        grad_normed = grad_normed + back_product(grad_kv_b, rows, QW, QW + 2 * KW, core)
        grad_front, grad_gain0 = jax.vjp(scaled_norm, kept["hidden_in"], gain_rows[0])[1](
            grad_normed
        )
        grad_hidden_b = (grad_hidden + grad_front).astype(BF)
        gain_vec = jnp.concatenate(
            [
                grad_gain0,
                grad_gain1,
                grad_gain2,
                grad_gain3,
                grad_gain4,
                grad_gain5,
                grad_query_gain,
                grad_key_gain,
            ]
        )
        late = jnp.concatenate([grad_q_b, grad_kv_b, grad_z_b], axis=1)
        return grad_hidden_b, late, ff_base, gain_vec

    near_0, near_1 = [], []
    out_0, kept_0 = forward(0, hidden_b, near_0)
    out_1, kept_1 = forward(1, out_0, near_1)
    normed_all_0 = lax.all_gather(kept_0["normed_b"], "shard", axis=0, tiled=True)
    top = pick(cotangent[0], cotangent[1])
    passed_0, passed_1, early_0, early_1, sides = [], [], [], [], []
    due_1 = [sides, normed_all_0, lambda work: work]
    grad_1, late_1, _, gain_vec_1 = backward(1, kept_1, top, passed_1, early_1, due_1)
    normed_all_0 = due_1[1]
    grad_1, normed_b = tie(grad_1, kept_1["normed_b"])
    normed_all_1 = lax.all_gather(normed_b, "shard", axis=0, tiled=True)

    def table_product(side_all):
        return dot_first(one_hot, side_all)

    def gather_sides():
        keep = pick(sides[1], sides[0])
        other = swap_cores(pick(sides[0], sides[1]))
        two = jnp.concatenate([pick(keep, other), pick(other, keep)], axis=0)
        return lax.all_gather(two, "shard", axis=0, tiled=True)

    due_0 = [sides, None, lambda work: (table_product(work[0]), work[1])]
    due_0_start = lambda: (gather_sides(), normed_all_1)
    due_0[1] = due_0_start
    grad_0, late_0, ff_base, gain_vec_0 = backward(0, kept_0, grad_1, passed_0, early_0, due_0)
    table_grad, normed_all_1 = due_0[1]

    def to_owners(late):
        padded = jnp.pad(late, ((0, 0), (0, n * rows_dev - IN_ROWS)))
        return padded.reshape(seq, n, rows_dev).transpose(1, 0, 2)

    gain_terms = jnp.concatenate(
        [gain_vec_0.reshape(n, gains_dev), gain_vec_1.reshape(n, gains_dev)], axis=1
    ).astype(BF)
    width = 2 * rows_dev
    gain_lines = -(-2 * gains_dev // width)
    gain_lines_padded = -(-gain_lines // 8) * 8
    gain_terms = jnp.pad(gain_terms, ((0, 0), (0, gain_lines_padded * width - 2 * gains_dev)))
    outgoing = jnp.concatenate(
        [
            jnp.concatenate([to_owners(late_0), to_owners(late_1)], axis=2),
            gain_terms.reshape(n, gain_lines_padded, width),
        ],
        axis=1,
    )
    incoming = lax.all_to_all(outgoing, "shard", 0, 0, tiled=True)
    background.drain()

    def finish_ff():
        passed = [
            jnp.concatenate([part[None] for part in parts], axis=0)
            for parts in (passed_0, passed_1)
        ]
        mine, theirs = pick(*passed), swap_cores(pick(passed[1], passed[0]))
        halves_in_order = jnp.concatenate([pick(mine, theirs), pick(theirs, mine)], axis=1)
        return ff_base + halves_in_order.astype(F32)

    def late_rows(arrived):
        sums = [
            dot_first(
                arrived[:, :seq, layer * rows_dev : (layer + 1) * rows_dev].reshape(
                    n * seq, rows_dev
                ),
                normed_all,
            )
            for layer, normed_all in enumerate((normed_all_0, normed_all_1))
        ]
        return pick(sums[0], sums[1]) + swap_cores(pick(sums[1], sums[0]).astype(BF)).astype(F32)

    ready, landed = [], []

    def finish(sent):
        if landed:
            passed_0.append(jnp.concatenate(landed, axis=0))
        ready.extend([finish_ff(), late_rows(incoming)])
        sent, ready[:] = tie(sent, list(ready))
        return sent

    run(early_rows(early_0.pop(), early_0, finish, last_pieces, landed))
    ff_grad, late_grad = ready
    early_keep = pick(early_0[0], early_1[0])
    early_other = swap_cores(pick(early_1[0], early_0[0]))
    attn_grad = (
        late_grad
        + rejoin(early_keep, early_other, core)
    )
    gain_sums = jnp.sum(incoming[:, seq:].astype(F32), axis=0).reshape(-1)
    gain_sums = (gain_sums[:gains_dev], gain_sums[gains_dev : 2 * gains_dev])
    gain_grad = pick(gain_sums[0], gain_sums[1]) + swap_cores(pick(gain_sums[1], gain_sums[0]))

    def outputs_of(value_0, value_1):
        keep = pick(value_0, value_1)
        other = swap_cores(pick(value_1, value_0))
        return jnp.stack([pick(keep, other), pick(other, keep)])

    return (
        outputs_of(out_0, out_1)[None],
        outputs_of(grad_0, grad_1)[None],
        attn_grad[None],
        ff_grad[None],
        gain_grad[None],
        table_grad[None],
    )


def solution(mesh):
    placed = (
        P(None, "shard", None),
        P(None, "shard", None),
        P(),
        P(None, "shard"),
        P("section", "shard", None),
        P("section", None, "shard", None),
        P("section", "shard"),
        P("section", "shard", None),
    )
    return jax.shard_map(
        per_device,
        mesh=mesh,
        in_specs=placed,
        out_specs=(
            P("section", None, "shard", None),
            P("section", None, "shard", None),
            P("section", "shard", None),
            P("section", None, "shard", None),
            P("section", "shard"),
            P("section", "shard", None),
        ),
        check_vma=False,
    )
```

```python
import itertools
import math
from functools import partial

import jax
import jax.numpy as jnp
from jax import lax
from jax.sharding import PartitionSpec as P

D = 2048
HEADS = 8
KV_HEADS = 2
HEAD_DIM = 256
RANK = 64
PLD = 256
HALF = D // 2
QW = HEADS * HEAD_DIM
KW = KV_HEADS * HEAD_DIM
IN_ROWS = QW + 2 * KW + RANK
OUT_START = IN_ROWS + PLD
LAUREL_START = OUT_START + QW
SIDE_START = LAUREL_START + RANK

EPS = 1e-06
ROPE_BASE = 10000.0
INV_ROOT2 = 0.7071067811865476
MASKED = -1e30
SCALE = HEAD_DIM ** (-0.5)
BF = jnp.bfloat16
F32 = jnp.float32

ALL_CHIPS = ((0, 2, 1), (0, 1, 2))
PLANE = ((0, 1), (0, 1))


def tie(*values):
    return lax.optimization_barrier(values)


def chip_dims(n):
    side = math.isqrt(n // 4)
    return (4, side, side)


def chip_strides(n):
    sizes = chip_dims(n)
    return (sizes[1] * sizes[2], sizes[2], 1)


def hop(value, n, dims, step):
    sizes, strides = chip_dims(n), chip_strides(n)
    pairs = []
    for core, dim in enumerate(dims):
        for i in range(n):
            place = (i // strides[dim]) % sizes[dim]
            target = i + ((place + step) % sizes[dim] - place) * strides[dim]
            pairs.append((core * n + i, core * n + target))
    return lax.ppermute(value, ("section", "shard"), pairs)


def swap_cores(value):
    return lax.ppermute(value, "section", [(0, 1), (1, 0)])


def offsets_of(n, orders):
    sizes = chip_dims(n)
    return list(itertools.product(*[range(sizes[d]) for d in orders[0]]))


def tree(n, orders):
    rounds = {}
    for offset in offsets_of(n, orders):
        if sum(offset) > 0:
            last = max(i for i, steps in enumerate(offset) if steps > 0)
            parent = tuple(steps - (i == last) for i, steps in enumerate(offset))
            edge = (offset, parent, (orders[0][last], orders[1][last]))
            rounds.setdefault(sum(offset), []).append(edge)
    return [rounds[number] for number in sorted(rounds)]


def source_index(me, core, n, orders, offset):
    sizes, strides = chip_dims(n), chip_strides(n)
    found = []
    for order in orders:
        index = me
        for dim, steps in zip(order, offset):
            place = (me // strides[dim]) % sizes[dim]
            index = index + ((place - steps) % sizes[dim] - place) * strides[dim]
        found.append(index)
    return jnp.where(core == 0, found[0], found[1])


def gather_tree(block, n, orders):
    found = {(0,) * len(orders[0]): block}
    for edges in tree(n, orders):
        for offset, parent, dims in edges:
            found[offset] = hop(found[parent], n, dims, 1)
    return found


def scatter_steps(terms, n, orders, sums, beside=None):
    totals = dict(terms)
    for number, edges in enumerate(reversed(tree(n, orders))):
        sent = [hop(totals[offset].astype(BF), n, dims, -1) for offset, _, dims in edges]
        if number == 1 and beside is not None:
            sent = beside(sent)
        sent, _ = yield sent
        for (_, parent, _), value in zip(edges, sent):
            totals[parent] = totals[parent].astype(F32) + value.astype(F32)
    sums.append(totals[(0,) * len(orders[0])])


def run(job):
    sent = next(job)
    while True:
        try:
            sent = job.send((sent, None))
        except StopIteration:
            return


def scatter_tree(terms, n, orders):
    sums = []
    run(scatter_steps(terms, n, orders, sums))
    return sums[0]


class Background:
    def __init__(self):
        self.jobs = []

    def add(self, job):
        self.jobs.append((job, next(job)))

    def stage(self, *values):
        values, flying = lax.optimization_barrier((values, [sent for _, sent in self.jobs]))
        going = []
        for (job, _), sent in zip(self.jobs, flying):
            try:
                going.append((job, job.send((sent, values[0]))))
            except StopIteration:
                pass
        self.jobs = going
        return values

    def drain(self):
        while self.jobs:
            going = []
            for job, sent in self.jobs:
                try:
                    going.append((job, job.send((sent, None))))
                except StopIteration:
                    pass
            self.jobs = going


def after(value, anchor):
    return value if anchor is None else tie(value, anchor)[0]


def gather_small(value, me, n):
    step = 1
    while step < n:
        other = lax.ppermute(value, "shard", [(i, i ^ step) for i in range(n)])
        lower = (me // step) % 2 == 0
        value = jnp.where(
            lower,
            jnp.concatenate([value, other], axis=0),
            jnp.concatenate([other, value], axis=0),
        )
        step *= 2
    return value


def rms_norm(values):
    return values * lax.rsqrt(jnp.mean(values * values, axis=-1, keepdims=True) + EPS)


def scaled_norm(values, gain_vec):
    return rms_norm(values) * gain_vec


def rope_tables(positions):
    half_width = HEAD_DIM // 2
    frequency = ROPE_BASE ** (-jnp.arange(half_width, dtype=F32) * (2.0 / HEAD_DIM))
    angles = positions.astype(F32)[:, None] * frequency[None, :]
    return (jnp.cos(angles), jnp.sin(angles))


def rotate(vectors, cosine_part, sine_part):
    half_width = vectors.shape[-1] // 2
    first_half = vectors[..., :half_width]
    second_half = vectors[..., half_width:]
    cosine_rows = cosine_part[:, None, :]
    sine_rows = sine_part[:, None, :]
    return jnp.concatenate(
        [
            first_half * cosine_rows - second_half * sine_rows,
            second_half * cosine_rows + first_half * sine_rows,
        ],
        axis=-1,
    )


def query_heads(projected, query_gain, cosine_part, sine_part):
    heads = projected.reshape(projected.shape[0], HEADS, HEAD_DIM)
    return rotate(rms_norm(heads) * query_gain, cosine_part, sine_part)


def key_value_heads(projected, key_gain, cosine_part, sine_part):
    row_count = projected.shape[0]
    key_heads = projected[:, :KW].reshape(row_count, KV_HEADS, HEAD_DIM)
    value_heads = projected[:, KW:].reshape(row_count, KV_HEADS, HEAD_DIM)
    key_heads = rotate(rms_norm(key_heads) * key_gain, cosine_part, sine_part)
    return jnp.concatenate(
        [key_heads.reshape(row_count, KW), rms_norm(value_heads).reshape(row_count, KW)], axis=1
    )


def join_piece(hidden_in, normed, attended, laurel_raw, gain_laurel, gain_attn, gain_ffin):
    joined = (
        hidden_in + rms_norm(attended) * gain_attn + normed + rms_norm(laurel_raw) * gain_laurel
    ) * INV_ROOT2
    return (joined, rms_norm(joined) * gain_ffin)


def gated_gelu(gate_pre, up_pre):
    return jax.nn.gelu(gate_pre, approximate=True) * up_pre


def add_branch(residual, branch, gain_out):
    return residual + rms_norm(branch) * gain_out


def dot(left_side, right_side):
    return jnp.dot(left_side, right_side, preferred_element_type=F32)


def dot_rows(left_side, right_side):
    return lax.dot_general(
        left_side, right_side, (((1,), (1,)), ((), ())), preferred_element_type=F32
    )


def dot_first(left_side, right_side):
    return lax.dot_general(
        left_side, right_side, (((0,), (0,)), ((), ())), preferred_element_type=F32
    )


def halves(value, core):
    left, right = value[..., :HALF], value[..., HALF:]
    return jnp.where(core == 0, left, right), jnp.where(core == 0, right, left)


def rejoin(own, other, core):
    return jnp.concatenate(
        [jnp.where(core == 0, own, other), jnp.where(core == 0, other, own)], axis=-1
    )


def rows_product(value, rows, start, stop, core):
    own, other = halves(value, core)
    return dot_rows(own, rows[0][start:stop]) + dot_rows(other, rows[1][start:stop])


def back_product(value, rows, start, stop, core):
    return rejoin(dot(value, rows[0][start:stop]), dot(value, rows[1][start:stop]), core)


def per_device(tokens, cotangent, block_ids, token_ids, attn_weight, ff_weight, gains, table):
    core = lax.axis_index("section")
    me = lax.axis_index("shard")
    n = lax.axis_size("shard")
    seq = tokens.shape[1]
    rows_dev = attn_weight.shape[1]
    units = ff_weight.shape[2]
    half_units = units // 2
    gains_dev = gains.shape[1]
    vocab_dev = table.shape[1]
    side = chip_dims(n)[2]
    background = Background()

    def pick(for_0, for_1):
        return jnp.where(core == 0, for_0, for_1)

    def by_layer(mine, theirs):
        return (pick(mine, theirs), pick(theirs, mine))

    gain_pair = by_layer(gains[0].astype(F32), swap_cores(gains[0]).astype(F32))
    small = jnp.concatenate([gain_pair[0], gain_pair[1], token_ids.reshape(-1).astype(F32)])
    small_all = gather_small(small[None], me, n)
    layer_gains = [
        small_all[:, layer * gains_dev : (layer + 1) * gains_dev].reshape(n * gains_dev)
        for layer in range(2)
    ]
    all_ids = small_all[:, 2 * gains_dev :].astype(jnp.int32).reshape(-1)

    one_hot = (
        (all_ids - me * vocab_dev)[:, None] == jnp.arange(vocab_dev, dtype=jnp.int32)[None, :]
    ).astype(BF)
    looked_up = dot(one_hot, table[0]).astype(BF)

    own_half, other_half = halves(attn_weight[0], core)
    attn_blocks = by_layer(own_half, swap_cores(other_half))
    rows_1_own = lax.all_gather(attn_blocks[1], "shard", axis=0, tiled=True)
    ff_own = by_layer(ff_weight[0], swap_cores(ff_weight[0]))
    ff_half = [lax.dynamic_slice_in_dim(own, core * half_units, half_units, 1) for own in ff_own]
    buffers = [jnp.zeros((n, rows_dev, HALF), BF), jnp.zeros((n, rows_dev, HALF), BF)]

    def store_blocks(buffers, fresh):
        for offset, block in fresh.items():
            sources = [source_index(me, c, n, ALL_CHIPS, offset) for c in (core, 1 - core)]
            buffers = [
                lax.dynamic_update_slice(
                    buffer, value[None], (source, jnp.int32(0), jnp.int32(0))
                )
                for buffer, value, source in zip(buffers, (block, swap_cores(block)), sources)
            ]
        return buffers

    fresh = {(0, 0, 0): attn_blocks[0]}
    held = dict(fresh)
    for number, edges in enumerate(tree(n, ALL_CHIPS)):
        arriving = {offset: hop(held[parent], n, dims, 1) for offset, parent, dims in edges}
        buffers = store_blocks(buffers, fresh)
        if number == 1:
            arriving, looked_up = tie(arriving, looked_up)
        if number == 2:
            arriving, ff_own = tie(arriving, ff_own)
        if number == 3:
            arriving, ff_half = tie(arriving, ff_half)
        fresh, held, buffers = tie(arriving, held, buffers)
        held.update(fresh)
    buffers = store_blocks(buffers, fresh)
    rows_0 = [buffer.reshape(n * rows_dev, HALF) for buffer in buffers]
    rows_1 = [rows_1_own, swap_cores(rows_1_own)]
    attn_rows = (rows_0, rows_1)
    looked_up = lax.psum_scatter(looked_up, "shard", scatter_dimension=0, tiled=True)
    looked_up = looked_up.reshape(2, seq, PLD)
    side_theirs = swap_cores(pick(looked_up[1], looked_up[0]))
    side_inputs = [
        value.astype(F32) for value in by_layer(pick(looked_up[0], looked_up[1]), side_theirs)
    ]

    positions = me * seq + jnp.arange(seq, dtype=jnp.int32)
    cosine_part, sine_part = rope_tables(positions)
    query_split = partial(query_heads, cosine_part=cosine_part, sine_part=sine_part)
    key_value_split = partial(key_value_heads, cosine_part=cosine_part, sine_part=sine_part)
    key_offsets = offsets_of(n, ALL_CHIPS)
    plane_offsets = offsets_of(n, PLANE)
    sources = jnp.stack([source_index(me, core, n, ALL_CHIPS, offset) for offset in key_offsets])
    blocks = pick(block_ids[0], block_ids[1]).reshape(n, seq)
    key_blocks = jnp.take(blocks, sources, axis=0).reshape(-1)
    allowed = key_blocks[None, :] <= key_blocks[:seq, None]
    hidden_b = pick(tokens[0], tokens[1])

    def near_units(layer, anchor, near):
        for which in range(3):
            current = after(ff_half[layer][which], anchor)
            parts = []
            for _ in range(side - 1):
                (current,), anchor = yield [hop(current, n, (2, 2), 1)]
                parts.append(current)
            near.append(parts)

    def plane_gather(value):
        found = gather_tree(value, n, PLANE)
        return jnp.concatenate([found[offset] for offset in plane_offsets], axis=0)

    def plane_scatter(value):
        terms = {o: value[i * seq : (i + 1) * seq] for i, o in enumerate(plane_offsets)}
        return scatter_tree(terms, n, PLANE)

    def split_gains(layer):
        flat = layer_gains[layer]
        return flat[: 6 * D].reshape(6, D), flat[6 * D : 6 * D + HEAD_DIM], flat[6 * D + HEAD_DIM :]

    def forward(layer, hidden_b, near):
        rows = attn_rows[layer]
        gain_rows, query_gain, key_gain = split_gains(layer)
        hidden_in = hidden_b.astype(F32)
        normed = scaled_norm(hidden_in, gain_rows[0])
        normed_b = normed.astype(BF)
        projected_kv = rows_product(normed_b, rows, QW, QW + 2 * KW, core)
        local = key_value_split(projected_kv, key_gain).astype(BF)
        (local,) = background.stage(local)
        if layer == 0:
            background.add(near_units(0, local, near))
        found = gather_tree(local, n, ALL_CHIPS)
        projected_q = rows_product(normed_b, rows, 0, QW, core)
        queries_b = query_split(projected_q, query_gain).astype(BF)
        queries_b = queries_b.reshape(seq, KV_HEADS, HEADS // KV_HEADS, HEAD_DIM)
        latent_b = rows_product(normed_b, rows, QW + 2 * KW, IN_ROWS, core).astype(BF)
        laurel_raw = back_product(latent_b, rows, LAUREL_START, SIDE_START, core)
        key_value = jnp.concatenate([found[offset] for offset in key_offsets], axis=0)
        key_value, queries_b, laurel_raw = background.stage(key_value, queries_b, laurel_raw)
        keys_b = key_value[:, :KW].reshape(-1, KV_HEADS, HEAD_DIM)
        values_b = key_value[:, KW:].reshape(-1, KV_HEADS, HEAD_DIM)
        scores = (
            jnp.einsum("qkgd,jkd->kgqj", queries_b, keys_b, preferred_element_type=F32) * SCALE
        )
        scores = jnp.where(allowed, scores, MASKED)
        row_max = jnp.max(scores, axis=-1, keepdims=True)
        exponentials = jnp.exp(scores - row_max)
        probabilities = exponentials / jnp.sum(exponentials, axis=-1, keepdims=True)
        mixed_b = (
            jnp.einsum(
                "kgqj,jkd->qkgd", probabilities.astype(BF), values_b, preferred_element_type=F32
            )
            .reshape(seq, QW)
            .astype(BF)
        )
        attended = back_product(mixed_b, rows, OUT_START, LAUREL_START, core)
        joined, prenorm = join_piece(
            hidden_in, normed, attended, laurel_raw, gain_rows[1], gain_rows[2], gain_rows[3]
        )
        (prenorm_b,) = background.stage(prenorm.astype(BF))
        prenorm_all = plane_gather(prenorm_b)
        (prenorm_all,) = background.stage(prenorm_all)
        while len(near) < 3:
            (prenorm_all,) = background.stage(prenorm_all)
        weights = [
            [ff_own[layer][which]]
            + [part for through in near[which] for part in (through, swap_cores(through))]
            for which in range(3)
        ]
        gate = [dot_rows(prenorm_all, part) for part in weights[0]]
        up = [dot_rows(prenorm_all, part) for part in weights[1]]
        hidden_ff_b = [gated_gelu(g, u).astype(BF) for g, u in zip(gate, up)]
        down_out = plane_scatter(sum(dot(h, part) for h, part in zip(hidden_ff_b, weights[2])))
        (down_out,) = background.stage(down_out)
        if layer == 0:
            background.add(near_units(1, down_out, near_1))
        settled = add_branch(joined, down_out, gain_rows[4])
        settled_b = settled.astype(BF)
        side_gate = rows_product(settled_b, rows, IN_ROWS, OUT_START, core)
        gated_b = gated_gelu(side_gate, side_inputs[layer]).astype(BF)
        projected = back_product(gated_b, rows, SIDE_START, SIDE_START + PLD, core)
        layer_out_b = add_branch(settled, projected, gain_rows[5]).astype(BF)
        return layer_out_b, dict(
            hidden_in=hidden_in,
            normed=normed,
            normed_b=normed_b,
            projected_q=projected_q,
            projected_kv=projected_kv,
            weights=weights,
            queries_b=queries_b,
            keys_b=keys_b,
            values_b=values_b,
            probabilities=probabilities,
            mixed_b=mixed_b,
            attended=attended,
            latent_b=latent_b,
            laurel_raw=laurel_raw,
            joined=joined,
            prenorm_all=prenorm_all,
            gate=gate,
            up=up,
            hidden_ff_b=hidden_ff_b,
            down_out=down_out,
            settled=settled,
            settled_b=settled_b,
            side_gate=side_gate,
            gated_b=gated_b,
            projected=projected,
        )

    def early_products(pairs):
        lefts = jnp.concatenate([left for left, _ in pairs], axis=1)
        lefts = jnp.concatenate([lefts, swap_cores(lefts)], axis=0)
        own, other = halves(jnp.stack([right for _, right in pairs]), core)
        rights = jnp.concatenate([own, swap_cores(other)], axis=1)
        terms = [jnp.zeros((IN_ROWS - upper_rows, HALF), BF)]
        start = 0
        for i, (left, _) in enumerate(pairs):
            stop = start + left.shape[1]
            terms.append(dot_first(lefts[:, start:stop], rights[i]).astype(BF))
            start = stop
        return jnp.concatenate(terms, axis=0)

    first = (rows_dev // 2 + 7) // 8 * 8
    upper_rows = n // 2 * rows_dev

    def early_rows(term, result, beside=None, finish=None):
        shaped = term.reshape(n // 2, rows_dev, HALF)
        upper = me >= n // 2
        pieces = {}
        for offset in key_offsets:
            target = source_index(me, core, n, ALL_CHIPS, offset)
            place = (target % (n // 2), jnp.where(target >= n // 2, 0, rows_dev - first), 0)
            pieces[offset] = lax.dynamic_slice(shaped, place, (1, first, HALF))[0]
        sums = []
        yield from scatter_steps(pieces, n, ALL_CHIPS, sums, beside)
        mine = sums[0].astype(BF)
        if finish is not None:
            mine = finish(mine)
        sent = lax.ppermute(mine, "shard", [(i, i + n // 2) for i in range(n // 2)])
        (sent,), _ = yield [sent]
        whole = jnp.concatenate([mine, sent[2 * first - rows_dev :]], axis=0).astype(F32)
        result.append(jnp.where(upper, whole, 0.0))

    def backward(layer, kept, grad_out_b, passed, early, due):
        rows = attn_rows[layer]
        weights = kept["weights"]
        gain_rows, query_gain, key_gain = split_gains(layer)
        grad_out = grad_out_b.astype(F32)
        grad_settled, grad_projected, grad_gain5 = jax.vjp(
            add_branch, kept["settled"], kept["projected"], gain_rows[5]
        )[1](grad_out)
        grad_projected_b = grad_projected.astype(BF)
        grad_gated = rows_product(grad_projected_b, rows, SIDE_START, SIDE_START + PLD, core)
        grad_side_gate, grad_side = jax.vjp(gated_gelu, kept["side_gate"], side_inputs[layer])[1](
            grad_gated
        )
        grad_side_gate_b = grad_side_gate.astype(BF)
        grad_settled = grad_settled + back_product(
            grad_side_gate_b, rows, IN_ROWS, OUT_START, core
        )
        grad_joined, grad_down, grad_gain4 = jax.vjp(
            add_branch, kept["joined"], kept["down_out"], gain_rows[4]
        )[1](grad_settled)
        due[0].append(grad_side.astype(BF))
        grad_down_b = grad_down.astype(BF)
        grad_down_all = plane_gather(grad_down_b)
        (grad_down_all,) = background.stage(grad_down_all)
        grad_hidden_ff = [dot_rows(grad_down_all, part) for part in weights[2]]
        grad_gate_up = [
            jax.vjp(gated_gelu, g, u)[1](grad)
            for g, u, grad in zip(kept["gate"], kept["up"], grad_hidden_ff)
        ]
        grad_gate_b = [pair[0].astype(BF) for pair in grad_gate_up]
        grad_up_b = [pair[1].astype(BF) for pair in grad_gate_up]
        grad_prenorm = sum(
            dot(g, wg) + dot(u, wu)
            for g, u, wg, wu in zip(grad_gate_b, grad_up_b, weights[0], weights[1])
        )
        grad_prenorm, grad_gate_b, grad_up_b = tie(grad_prenorm, grad_gate_b, grad_up_b)
        grad_prenorm = plane_scatter(grad_prenorm)
        ff_terms = [
            [dot_first(g, kept["prenorm_all"]).astype(BF) for g in grad_gate_b],
            [dot_first(u, kept["prenorm_all"]).astype(BF) for u in grad_up_b],
            [dot_first(h, grad_down_all).astype(BF) for h in kept["hidden_ff_b"]],
        ]
        ff_base = jnp.stack([terms[0] for terms in ff_terms])
        pair_sums = [
            [
                (terms[1 + 2 * i].astype(F32) + swap_cores(terms[2 + 2 * i]).astype(F32)).astype(BF)
                for i in range(side - 1)
            ]
            for terms in ff_terms
        ]
        grad_prenorm, pair_sums, ff_base = background.stage(grad_prenorm, pair_sums, ff_base)

        def pass_back():
            anchor = None
            for which in range(3):
                carried = None
                for steps in range(side - 1, 0, -1):
                    term = after(pair_sums[which][steps - 1], anchor)
                    if carried is not None:
                        term = (term.astype(F32) + carried.astype(F32)).astype(BF)
                    (carried,), anchor = yield [hop(term, n, (2, 2), -1)]
                passed.append(carried)

        background.add(pass_back())
        join_pull = jax.vjp(
            join_piece,
            kept["hidden_in"],
            kept["normed"],
            kept["attended"],
            kept["laurel_raw"],
            gain_rows[1],
            gain_rows[2],
            gain_rows[3],
        )[1]
        grad_hidden, grad_normed, grad_attended, grad_laurel, grad_gain1, grad_gain2, grad_gain3 = (
            join_pull((grad_joined, grad_prenorm))
        )
        grad_attended_b = grad_attended.astype(BF)
        grad_laurel_b = grad_laurel.astype(BF)
        grad_mixed_b = rows_product(grad_attended_b, rows, OUT_START, LAUREL_START, core).astype(BF)
        grad_latent = rows_product(grad_laurel_b, rows, LAUREL_START, SIDE_START, core)
        grad_mixed_heads = grad_mixed_b.reshape(seq, KV_HEADS, HEADS // KV_HEADS, HEAD_DIM)
        probabilities = kept["probabilities"]
        grad_probs = jnp.einsum(
            "qkgd,jkd->kgqj", grad_mixed_heads, kept["values_b"], preferred_element_type=F32
        )
        row_dot = jnp.sum(grad_probs * probabilities, axis=-1, keepdims=True)
        grad_scores_b = (probabilities * (grad_probs - row_dot)).astype(BF)
        grad_keys_all = (
            jnp.einsum(
                "kgqj,qkgd->jkd", grad_scores_b, kept["queries_b"], preferred_element_type=F32
            )
            * SCALE
        )
        grad_values_all = jnp.einsum(
            "kgqj,qkgd->jkd",
            probabilities.astype(BF),
            grad_mixed_heads,
            preferred_element_type=F32,
        )
        grad_key_value = jnp.concatenate(
            [grad_keys_all.reshape(-1, KW), grad_values_all.reshape(-1, KW)], axis=1
        ).astype(BF)
        early_pairs = (
            (grad_side_gate_b, kept["settled_b"]),
            (kept["mixed_b"], grad_attended_b),
            (kept["latent_b"], grad_laurel_b),
            (kept["gated_b"], grad_projected_b),
        )
        work = due[1]() if callable(due[1]) else due[1]
        grad_key_value, early_pairs, work = background.stage(grad_key_value, early_pairs, work)
        early_term = early_products(early_pairs)
        due[1] = due[2](work)
        terms = {o: grad_key_value[i * seq : (i + 1) * seq] for i, o in enumerate(key_offsets)}
        grad_local = scatter_tree(terms, n, ALL_CHIPS)
        grad_queries = (
            jnp.einsum("kgqj,jkd->qkgd", grad_scores_b, kept["keys_b"], preferred_element_type=F32)
            * SCALE
        )
        grad_projected_q, grad_query_gain = jax.vjp(query_split, kept["projected_q"], query_gain)[
            1
        ](grad_queries.reshape(seq, HEADS, HEAD_DIM))
        grad_q_b, grad_z_b = grad_projected_q.astype(BF), grad_latent.astype(BF)
        grad_normed = (
            grad_normed
            + back_product(grad_q_b, rows, 0, QW, core)
            + back_product(grad_z_b, rows, QW + 2 * KW, IN_ROWS, core)
        )
        grad_local, grad_normed, early_term, due[1] = background.stage(
            grad_local, grad_normed, early_term, due[1]
        )
        if layer == 1:
            background.add(early_rows(early_term, early))
        else:
            early.append(early_term)
        grad_projected_kv, grad_key_gain = jax.vjp(
            key_value_split, kept["projected_kv"], key_gain
        )[1](grad_local)
        grad_kv_b = grad_projected_kv.astype(BF)
        grad_normed = grad_normed + back_product(grad_kv_b, rows, QW, QW + 2 * KW, core)
        grad_front, grad_gain0 = jax.vjp(scaled_norm, kept["hidden_in"], gain_rows[0])[1](
            grad_normed
        )
        grad_hidden_b = (grad_hidden + grad_front).astype(BF)
        gain_vec = jnp.concatenate(
            [
                grad_gain0,
                grad_gain1,
                grad_gain2,
                grad_gain3,
                grad_gain4,
                grad_gain5,
                grad_query_gain,
                grad_key_gain,
            ]
        )
        late = jnp.concatenate([grad_q_b, grad_kv_b, grad_z_b], axis=1)
        return grad_hidden_b, late, ff_base, gain_vec

    near_0, near_1 = [], []
    out_0, kept_0 = forward(0, hidden_b, near_0)
    out_1, kept_1 = forward(1, out_0, near_1)
    normed_all_0 = lax.all_gather(kept_0["normed_b"], "shard", axis=0, tiled=True)
    top = pick(cotangent[0], cotangent[1])
    passed_0, passed_1, early_0, early_1, sides = [], [], [], [], []
    due_1 = [sides, normed_all_0, lambda work: work]
    grad_1, late_1, ff_base_1, gain_vec_1 = backward(1, kept_1, top, passed_1, early_1, due_1)
    normed_all_0 = due_1[1]
    grad_1, normed_b = tie(grad_1, kept_1["normed_b"])
    normed_all_1 = lax.all_gather(normed_b, "shard", axis=0, tiled=True)

    def table_product(side_all):
        return dot_first(one_hot, side_all)

    def gather_sides():
        keep = pick(sides[1], sides[0])
        other = swap_cores(pick(sides[0], sides[1]))
        two = jnp.concatenate([pick(keep, other), pick(other, keep)], axis=0)
        return lax.all_gather(two, "shard", axis=0, tiled=True)

    due_0 = [sides, None, lambda work: (table_product(work[0]), work[1])]
    due_0_start = lambda: (gather_sides(), normed_all_1)
    due_0[1] = due_0_start
    grad_0, late_0, ff_base_0, gain_vec_0 = backward(0, kept_0, grad_1, passed_0, early_0, due_0)
    table_grad, normed_all_1 = due_0[1]

    def to_owners(late):
        padded = jnp.pad(late, ((0, 0), (0, n * rows_dev - IN_ROWS)))
        return padded.reshape(seq, n, rows_dev).transpose(1, 0, 2)

    gain_terms = jnp.concatenate(
        [gain_vec_0.reshape(n, gains_dev), gain_vec_1.reshape(n, gains_dev)], axis=1
    ).astype(BF)
    width = 2 * rows_dev
    gain_lines = -(-2 * gains_dev // width)
    gain_lines_padded = -(-gain_lines // 8) * 8
    gain_terms = jnp.pad(gain_terms, ((0, 0), (0, gain_lines_padded * width - 2 * gains_dev)))
    outgoing = jnp.concatenate(
        [
            jnp.concatenate([to_owners(late_0), to_owners(late_1)], axis=2),
            gain_terms.reshape(n, gain_lines_padded, width),
        ],
        axis=1,
    )
    incoming = lax.all_to_all(outgoing, "shard", 0, 0, tiled=True)
    background.drain()

    def whole_ff(base, passed):
        passed = jnp.concatenate([part[None] for part in passed], axis=0)
        zeros = jnp.zeros((3, units - half_units, D), BF)
        placed = pick(
            jnp.concatenate([passed, zeros], axis=1), jnp.concatenate([zeros, passed], axis=1)
        )
        return base.astype(F32) + placed.astype(F32)

    def finish_ff(base_0, passed_0, base_1, passed_1):
        whole_0, whole_1 = whole_ff(base_0, passed_0), whole_ff(base_1, passed_1)
        other = swap_cores(pick(whole_1, whole_0).astype(BF)).astype(F32)
        return pick(whole_0, whole_1) + other

    def late_rows(arrived):
        sums = [
            dot_first(
                arrived[:, :seq, layer * rows_dev : (layer + 1) * rows_dev].reshape(
                    n * seq, rows_dev
                ),
                normed_all,
            )
            for layer, normed_all in enumerate((normed_all_0, normed_all_1))
        ]
        return pick(sums[0], sums[1]) + swap_cores(pick(sums[1], sums[0]).astype(BF)).astype(F32)

    ready = []

    def beside(sent):
        sent, parts = tie(sent, (ff_base_0, passed_0, ff_base_1, passed_1))
        ready.append(finish_ff(*parts))
        return sent

    def finish(mine):
        ready.append(late_rows(incoming))
        mine, ready[:] = tie(mine, list(ready))
        return mine

    run(early_rows(early_0.pop(), early_0, beside, finish))
    ff_grad, late_grad = ready
    early_keep = pick(early_0[0], early_1[0])
    early_other = swap_cores(pick(early_1[0], early_0[0]))
    attn_grad = (
        late_grad
        + rejoin(early_keep, early_other, core)
    )
    gain_sums = jnp.sum(incoming[:, seq:].astype(F32), axis=0).reshape(-1)
    gain_sums = (gain_sums[:gains_dev], gain_sums[gains_dev : 2 * gains_dev])
    gain_grad = pick(gain_sums[0], gain_sums[1]) + swap_cores(pick(gain_sums[1], gain_sums[0]))

    def outputs_of(value_0, value_1):
        keep = pick(value_0, value_1)
        other = swap_cores(pick(value_1, value_0))
        return jnp.stack([pick(keep, other), pick(other, keep)])

    return (
        outputs_of(out_0, out_1)[None],
        outputs_of(grad_0, grad_1)[None],
        attn_grad[None],
        ff_grad[None],
        gain_grad[None],
        table_grad[None],
    )


def solution(mesh):
    placed = (
        P(None, "shard", None),
        P(None, "shard", None),
        P(),
        P(None, "shard"),
        P("section", "shard", None),
        P("section", None, "shard", None),
        P("section", "shard"),
        P("section", "shard", None),
    )
    return jax.shard_map(
        per_device,
        mesh=mesh,
        in_specs=placed,
        out_specs=(
            P("section", None, "shard", None),
            P("section", None, "shard", None),
            P("section", "shard", None),
            P("section", None, "shard", None),
            P("section", "shard"),
            P("section", "shard", None),
        ),
        check_vma=False,
    )
```
